128 devices in a mesh: slab: 16 (over z, y_lo, core), coil: 8 (over y_hi, x).
Axes of the slice: x: 4, y: 4 (y_hi: 2, y_lo: 2; y = y_hi * 2 + y_lo), z: 4, core: 2. Of those that a mesh axis runs over, the one named last changes fastest.
Arguments:
- image: float32 [2, 128, 128, 128], P(None, 'slab'), may hold values from -6 to 6
- cotangent: float32 [2, 128, 128, 128], P(None, 'slab'), may hold values from -6 to 6
- sens: float32 [16, 2, 128, 128, 128], P('coil', None, 'slab'), may hold values from -6 to 6
- mask: int32 [128, 128], replicated, may hold values 0 or 1
- labels: int32 [128, 64, 64], P('slab'), may hold values from 0 to 1
- embed_weight: float32 [8, 96], replicated, may hold values from -2 to 2
- ln_gain: float32 [96], replicated, may hold values from 0.1 to 1.9
- qkv_weight: bfloat16 [96, 288], replicated, may hold values from -8 to 8
- proj_weight: bfloat16 [96, 96], replicated, may hold values from -0.625 to 0.625
- unembed_weight: float32 [96, 8], replicated, may hold values from -0.625 to 0.625
Outputs:
- image_grad: float32 [2, 128, 128, 128], P(None, 'slab')
The draws below stay inside these ranges and needn't reach their ends.
All inputs are finite; a program needn't handle non-finite values.
Results may differ from the reference program's by a relative error of at most 0.028.
The reference program's roundings to bfloat16 on the way (of `normed`, `projected`, `attention` and `attended`) count: a program that leaves them out, or rounds other values in their place, can miss the bound.
Values sent between devices are 32-bit elements; how exact they have to be, the bound alone decides.
A program may use at most 64 MiB of HBM per device.

```python
import jax
import jax.numpy as jnp
from jax import lax

NX = 128
NY = 128
WIN = 8
SHIFT = 4
PATCH = 2
CH = 96
HEADS = 3
HD = 32
FEAT = 8
NZ = 128
COILS = 16


def draw_qkv_weight(key, part):
    key = jax.random.fold_in(key, 17)
    spread = CH ** (-0.5)
    values = jax.random.truncated_normal(key, -6.0, 6.0, (CH, 3 * CH), jnp.float32) * spread
    return values.astype(jnp.bfloat16)


def place_ends(drawn, key, smallest, largest):
    dims = drawn.shape
    index_at = [jax.random.randint(jax.random.fold_in(key, axis), (), 0, dims[axis]) for axis in range(len(dims))]
    drawn = drawn.at[tuple(index_at)].set(smallest)
    longest = dims.index(max(dims))
    index_at[longest] = (index_at[longest] + 1) % dims[longest]
    return drawn.at[tuple(index_at)].set(largest)


def levels(stream_key, dims, shards, smallest, high):
    factor_of, own = 1.0, jax.random.fold_in(stream_key, 6)
    for axis_at, blocks in shards:
        steps = jnp.exp(jax.random.uniform(jax.random.fold_in(own, axis_at), (blocks,), jnp.float32, smallest / len(shards), high / len(shards)))
        factor_of = factor_of * jnp.repeat(steps, dims[axis_at] // blocks).reshape([-1 if axis == axis_at else 1 for axis in range(len(dims))])
    return factor_of


def gaussian(rng, dims, width, limit, shards=(), held_as=jnp.bfloat16):
    drawn = width * jax.random.normal(rng, dims, jnp.float32)
    if shards:
        drawn = drawn * levels(rng, dims, shards, -0.22, 0.18)
    return jnp.clip(drawn, -limit, limit).astype(held_as)


def setup_inputs(seed: int = 0) -> dict:
    key_of = jax.random.split(jax.random.key(seed), 11)
    return {
        "image": gaussian(key_of[0], (2, NZ, NX, NY), 1.0, 6.0, ((1, 16),), jnp.float32),
        "cotangent": gaussian(key_of[1], (2, NZ, NX, NY), 1.0, 6.0, ((1, 16),), jnp.float32),
        "sens": gaussian(key_of[2], (COILS, 2, NZ, NX, NY), 0.5, 6.0, ((0, 8), (2, 16)), jnp.float32),
        "mask": place_ends((jax.random.randint(key_of[3], (NZ, NY), 0, 3) < 1).astype(jnp.int32), jax.random.fold_in(key_of[3], 1), 0, 1),
        "labels": place_ends(jax.random.randint(key_of[4], (NZ, NX // PATCH, NY // PATCH), 0, 2), jax.random.fold_in(key_of[4], 1), 0, 1).astype(jnp.int32),
        "embed_weight": gaussian(key_of[5], (FEAT, CH), FEAT ** -0.5, 2.0, (), jnp.float32),
        "ln_gain": jnp.clip(1.0 + 0.18 * jax.random.normal(key_of[6], (CH,), jnp.float32), 0.1, 1.9),
        "qkv_weight": draw_qkv_weight(jax.random.fold_in(key_of[10], 71), 0),
        "proj_weight": gaussian(key_of[8], (CH, CH), CH ** -0.5, 0.625),
        "unembed_weight": gaussian(key_of[9], (CH, FEAT), CH ** -0.5, 0.625, (), jnp.float32),
    }


STEP_SIZE = 0.5
NORM_EPSILON = 1e-05
HIGHEST_PRECISION = lax.Precision.HIGHEST

def to_windows(field):
    parts, planes, width_x, width_y = field.shape
    across_x = width_x // (PATCH * WIN)
    across_y = width_y // (PATCH * WIN)
    reshaped = field.reshape(parts, planes, across_x, WIN, PATCH, across_y, WIN, PATCH)
    reshaped = reshaped.transpose(2, 5, 1, 3, 6, 0, 4, 7)
    return reshaped.reshape(across_x * across_y, planes * WIN * WIN, parts * PATCH * PATCH)

def from_windows(tokens, shape):
    parts, planes, width_x, width_y = shape
    across_x = width_x // (PATCH * WIN)
    across_y = width_y // (PATCH * WIN)
    reshaped = tokens.reshape(across_x, across_y, planes, WIN, WIN, parts, PATCH, PATCH)
    reshaped = reshaped.transpose(5, 2, 0, 3, 6, 1, 4, 7)
    return reshaped.reshape(shape)

def label_windows(token_labels):
    planes, width_x, width_y = token_labels.shape
    across_x = width_x // WIN
    across_y = width_y // WIN
    reshaped = token_labels.reshape(planes, across_x, WIN, across_y, WIN)
    return reshaped.transpose(1, 3, 0, 2, 4).reshape(across_x * across_y, planes * WIN * WIN)

def attend(features, token_labels, embed_weight, ln_gain, qkv_weight, proj_weight, unembed_weight):
    tokens_count = features.shape[0]
    embedded = jnp.dot(features, embed_weight, precision=HIGHEST_PRECISION, preferred_element_type=jnp.float32)
    feature_mean = lax.optimization_barrier(jnp.mean(embedded, -1, keepdims=True))
    centered = embedded - feature_mean
    variance = lax.optimization_barrier(jnp.mean(centered * centered, -1, keepdims=True))
    normed = (centered * lax.rsqrt(variance + NORM_EPSILON) * ln_gain).astype(jnp.bfloat16)
    projected = jnp.dot(normed, qkv_weight, preferred_element_type=jnp.float32).astype(jnp.bfloat16)
    projected = projected.reshape(tokens_count, 3, HEADS, HD).astype(jnp.float32)
    scores = jnp.einsum('qhd,khd->hqk', projected[:, 0], projected[:, 1]) * HD ** (-0.5)
    same_label = token_labels[:, None] == token_labels[None, :]
    scores = jnp.where(same_label[None], scores, -1000000000.0)
    row_max = lax.optimization_barrier(jnp.max(scores, -1, keepdims=True))
    weights = jnp.exp(scores - row_max)
    attention = (weights / lax.optimization_barrier(jnp.sum(weights, -1, keepdims=True))).astype(jnp.bfloat16)
    attended = jnp.einsum('hqk,khd->qhd', attention.astype(jnp.float32), projected[:, 2])
    attended = attended.astype(jnp.bfloat16).reshape(tokens_count, CH)
    mixed_sum = embedded + jnp.dot(attended, proj_weight, preferred_element_type=jnp.float32)
    return jnp.dot(mixed_sum, unembed_weight, precision=HIGHEST_PRECISION, preferred_element_type=jnp.float32)

def reference(image, cotangent, sens, mask, labels, embed_weight, ln_gain, qkv_weight, proj_weight, unembed_weight):
    sens_real = sens[:, 0]
    sens_imag = sens[:, 1]
    grad_real = cotangent[0]
    grad_imag = cotangent[1]
    sensed = sens_real * grad_real - sens_imag * grad_imag + 1j * (sens_real * grad_imag + sens_imag * grad_real)
    kspace = jnp.fft.fftn(sensed, axes=(1, 2, 3), norm='ortho')
    kept_mask = mask.astype(jnp.float32)[:, None, :]
    returned = jnp.fft.ifftn(kspace * kept_mask, axes=(1, 2, 3), norm='ortho')
    back_real = jnp.real(returned).astype(jnp.float32)
    back_imag = jnp.imag(returned).astype(jnp.float32)
    consistency = jnp.stack([lax.optimization_barrier(jnp.sum(sens_real * back_real + sens_imag * back_imag, 0)), lax.optimization_barrier(jnp.sum(sens_real * back_imag - sens_imag * back_real, 0))])
    offset = SHIFT * PATCH
    shifted_image = jnp.roll(image, (-SHIFT, -offset, -offset), axis=(1, 2, 3))
    shifted_grad = jnp.roll(cotangent, (-SHIFT, -offset, -offset), axis=(1, 2, 3))

    def one_window(inputs):
        features, cotangents, token_labels = inputs

        def forward(values):
            return attend(values, token_labels, embed_weight, ln_gain, qkv_weight, proj_weight, unembed_weight)
        outputs, pullback = jax.vjp(forward, features)
        return pullback(cotangents)[0]

    def one_slab(slab_index):
        start_plane = (slab_index * WIN).astype(jnp.int32)
        slab_field = lax.dynamic_slice_in_dim(shifted_image, start_plane, WIN, 1)
        slab_grad = lax.dynamic_slice_in_dim(shifted_grad, start_plane, WIN, 1)
        slab_labels = lax.dynamic_slice_in_dim(labels, start_plane, WIN, 0)
        grads = lax.map(one_window, (to_windows(slab_field), to_windows(slab_grad), label_windows(slab_labels)))
        return from_windows(grads, slab_field.shape)
    slab_grads = lax.map(one_slab, jnp.arange(NZ // WIN, dtype=jnp.int32))
    swin_grad = jnp.moveaxis(slab_grads, 0, 1).reshape(2, NZ, NX, NY)
    swin_grad = jnp.roll(swin_grad, (SHIFT, offset, offset), axis=(1, 2, 3))
    return cotangent - STEP_SIZE * consistency + swin_grad
```

```python
import functools

import jax
import jax.numpy as jnp
import numpy as np
from jax import lax
from jax.experimental import pallas as pl
from jax.experimental.pallas import tpu as pltpu
from jax.sharding import PartitionSpec as P

MESH = pl.DeviceIdType.MESH
F32 = jnp.float32
BF16 = jnp.bfloat16
HEADS = 3
HEAD = 32
CHANNELS = 96
WINDOWS = 8
TOKENS = 512
GROUPS = 4
CHUNK = 256
EPSILON = 1e-5
STEP_SIZE = 0.5
SCALE = HEAD ** -0.5
PENALTY = 1e9


def dft_tables(length):
    index = np.arange(length)
    angle = (index[:, None] * index[None, :] % length) * (2.0 * np.pi / length)
    cos = np.cos(angle) / np.sqrt(length)
    sin = np.sin(angle) / np.sqrt(length)
    forward = np.block([[cos, sin], [-sin, cos]])
    high = forward.astype(jnp.bfloat16)
    low = (forward - high.astype(np.float64)).astype(jnp.bfloat16)
    return np.stack([high, low, np.ascontiguousarray(high.T), np.ascontiguousarray(low.T)])


def selections():
    select = np.zeros((GROUPS, 8, 32), np.float32)
    for t in range(GROUPS):
        for f in range(8):
            part, px, py = f // 4, f // 2 % 2, f % 2
            select[t, f, part * 16 + px * 8 + 2 * t + py] = 1.0
    wide = np.zeros((3, GROUPS, 8, 192), np.float32)
    for slot, piece in enumerate((0, 0, 0, 1, 1, 2)):
        wide[piece, :, :, 32 * slot : 32 * slot + 32] = select
    return wide, np.ascontiguousarray(select.transpose(0, 2, 1))


def dot(left, right):
    return jnp.dot(left, right, preferred_element_type=F32)


def split2(value):
    high = value.astype(BF16)
    return high, (value - high.astype(F32)).astype(BF16)


def split3(value):
    high = value.astype(BF16)
    rest = value - high.astype(F32)
    middle = rest.astype(BF16)
    return high, middle, (rest - middle.astype(F32)).astype(BF16)


def lane_index(shape):
    return lax.broadcasted_iota(jnp.int32, shape, len(shape) - 1)


def prepare_weights(w):
    wide, narrow = w.wide, w.narrow
    emb = w.embed[...]
    w.pad[...] = jnp.zeros((128, 384), F32)
    w.pad[0:8, 0:CHANNELS] = emb
    w.pad[8:16, 0:CHANNELS] = jnp.broadcast_to(w.gain[...], (8, CHANNELS))
    turned = jnp.transpose(w.pad[:, 0:128])
    w.gain_col[...] = jnp.broadcast_to(turned[0:CHANNELS, 8:9], (CHANNELS, 128))
    emb_t = split3(turned[0:CHANNELS, 0:8])
    un = split3(w.unembed[...])
    emb_pieces = split2(emb)
    for t in range(GROUPS):
        w.to_embed[t] = sum(dot(p.astype(F32), wide[i, t]) for i, p in enumerate(emb_t)).astype(BF16)
        w.to_mixed[t] = sum(dot(p.astype(F32), wide[i, t]) for i, p in enumerate(un)).astype(BF16)
        for i, p in enumerate(emb_pieces):
            w.from_embed[i, t] = dot(narrow[t], p.astype(F32)).astype(BF16)
    w.pad[0:CHANNELS, 0:288] = w.qkv[...].astype(F32)
    for b in range(3):
        w.qkv_t[128 * b : 128 * b + 128, :] = jnp.transpose(w.pad[:, 128 * b : 128 * b + 128]).astype(BF16)


def prepare_fields(col, lab, w):
    rows = col.reshape(2, 2, 128, 128)
    low = lane_index((8, 128)) < 64
    for part in range(2):
        for px in range(2):
            both = jnp.concatenate(
                [rows[arr, part, pl.ds(px, 64, stride=2), :] for arr in range(2)], 0
            )
            w.turn[...] = jnp.transpose(both)
            place = 8 * (part * 2 + px)
            for win in range(WINDOWS):
                first = w.turn[8 * ((2 * win + 1) % 16) : 8 * ((2 * win + 1) % 16) + 8, :]
                second = w.turn[8 * ((2 * win + 2) % 16) : 8 * ((2 * win + 2) % 16) + 8, :]
                w.field[win, 0, place : place + 8, :] = jnp.where(low, first, pltpu.roll(second, 64, 1))
                w.field[win, 1, place : place + 8, :] = jnp.where(low, pltpu.roll(first, 64, 1), second)
    w.pad[:, 0:128] = jnp.zeros((128, 128), F32)
    for z in range(8):
        w.pad[8 * z : 8 * z + 8, 0:64] = lab[z].astype(F32)
    w.turn[...] = jnp.transpose(w.pad[:, 0:128])
    for win in range(WINDOWS):
        tile = w.turn[8 * win : 8 * win + 8, :]
        moved = pltpu.roll(pltpu.roll(tile, 4, 0), 64, 1)
        w.label[win] = jnp.where(low, tile, moved)


def one_window(win, w):
    image6 = split3(w.field[win, 0])
    grad6 = split3(w.field[win, 1])
    order = (0, 1, 2, 0, 1, 0)
    image6 = jnp.concatenate([image6[i] for i in order], 0)
    grad6 = jnp.concatenate([grad6[i] for i in order], 0)
    embedded = jnp.concatenate([dot(w.to_embed[t], image6) for t in range(GROUPS)], 1)
    mixed = jnp.concatenate([dot(w.to_mixed[t], grad6) for t in range(GROUPS)], 1)
    label = w.label[win]
    label = jnp.concatenate([label[t : t + 1, :] for t in range(GROUPS)], 1)

    gain = jnp.concatenate([w.gain_col[...]] * GROUPS, 1)
    mean = jnp.sum(embedded, 0, keepdims=True) * (1.0 / CHANNELS)
    centered = embedded - mean
    variance = jnp.sum(centered * centered, 0, keepdims=True) * (1.0 / CHANNELS)
    inverse = lax.rsqrt(variance + EPSILON)
    unit = centered * inverse
    w.unit[...] = unit
    normed = (unit * gain).astype(BF16)
    projected = dot(w.qkv_t[0:288, :][:, 0:CHANNELS], normed).astype(BF16).astype(F32)
    proj = w.proj[...]
    mixed_high, mixed_low = split2(mixed)
    attended = (dot(proj, mixed_high) + dot(proj, mixed_low)).astype(BF16).astype(F32)
    w.mixed[...] = mixed

    row = lax.broadcasted_iota(jnp.int32, (HEAD, TOKENS), 0)
    zero_f = jnp.zeros((HEAD, TOKENS), F32)
    zero = zero_f.astype(BF16)
    label_key = jnp.where(row == 0, label, jnp.where(row == 1, 1.0 - label, 0.0))
    label_query = jnp.where(row == 0, label - 1.0, jnp.where(row == 1, -label, 0.0)) * PENALTY
    label_query = label_query.astype(BF16)
    lane = lane_index((1, 128))
    only_query = ((lane >= 64) & (lane < 96)).astype(F32)
    only_grad = (lane >= 96).astype(F32)
    lane_scale = jnp.where(lane < 96, SCALE, 1.0).astype(F32)

    for head in range(HEADS):
        at = HEAD * head
        query = projected[at : at + HEAD]
        key = projected[CHANNELS + at : CHANNELS + at + HEAD]
        value = projected[2 * CHANNELS + at : 2 * CHANNELS + at + HEAD]
        grad = attended[at : at + HEAD]
        token = jnp.transpose(jnp.concatenate([key, value, query, grad], 0))
        more = jnp.transpose(jnp.concatenate([key, key, label_key, zero_f], 0))
        token_query = (token * only_query).astype(BF16)
        token_grad = (token * only_grad).astype(BF16)
        token = token.astype(BF16)
        left = jnp.concatenate([token, more.astype(BF16)], 1)
        parts = split3(query * (SCALE * float(np.log2(np.e))))
        right = jnp.concatenate(
            [parts[0], zero, zero, zero, parts[1], parts[2], label_query, zero], 0
        )
        right_value = jnp.concatenate([zero, grad.astype(BF16), zero, zero], 0)
        key16 = key.astype(BF16)
        total = jnp.zeros((TOKENS, 128), F32)
        for chunk in range(TOKENS // CHUNK):
            cut = slice(CHUNK * chunk, CHUNK * chunk + CHUNK)
            scores = dot(left, right[:, cut])
            top = jnp.max(scores, 0, keepdims=True)
            weights = jnp.exp2(scores - top)
            soft = weights * (1.0 / jnp.sum(weights, 0, keepdims=True))
            d_soft = dot(token, right_value[:, cut]).astype(BF16).astype(F32)
            inner = jnp.sum(d_soft * soft, 0, keepdims=True)
            d_scores = (soft * (d_soft - inner)).astype(BF16)
            w.d_proj[at : at + HEAD, cut] = dot(key16, d_scores) * SCALE
            total = total + dot(soft.astype(BF16), token_grad[cut, :]) + dot(d_scores, token_query[cut, :])
        total = jnp.transpose(total * lane_scale)
        w.d_proj[CHANNELS + at : CHANNELS + at + HEAD, :] = total[64:96]
        w.d_proj[2 * CHANNELS + at : 2 * CHANNELS + at + HEAD, :] = total[96:128]

    d_normed = dot(w.qkv[...], w.d_proj[...].astype(BF16)).astype(BF16).astype(F32)
    d_unit = d_normed * gain
    unit = w.unit[...]
    first = jnp.sum(d_unit, 0, keepdims=True) * (1.0 / CHANNELS)
    second = jnp.sum(d_unit * unit, 0, keepdims=True) * (1.0 / CHANNELS)
    d_embedded = inverse * (d_unit - first - unit * second) + w.mixed[...]
    high, low = split2(d_embedded)
    result = jnp.zeros((32, 128), F32)
    for t in range(GROUPS):
        cut = slice(128 * t, 128 * t + 128)
        result += dot(w.from_embed[0, t], high[:, cut])
        result += dot(w.from_embed[0, t], low[:, cut])
        result += dot(w.from_embed[1, t], high[:, cut])
    w.d_field[win] = result


def finish_fields(piece, w):
    rows = piece.reshape(2, 128, 128)
    low = lane_index((8, 128)) < 64
    for px in range(2):
        for win in range(WINDOWS):
            real = w.d_field[win, 8 * px : 8 * px + 8, :]
            imag = w.d_field[win, 16 + 8 * px : 24 + 8 * px, :]
            first = 8 * ((2 * win + 1) % 16)
            second = 8 * ((2 * win + 2) % 16)
            w.turn[first : first + 8, :] = jnp.where(low, real, pltpu.roll(imag, 64, 1))
            w.turn[second : second + 8, :] = jnp.where(low, pltpu.roll(real, 64, 1), imag)
        turned = jnp.transpose(w.turn[...])
        for part in range(2):
            rows[part, pl.ds(px, 64, stride=2), :] = turned[64 * part : 64 * part + 64, :]


def product3(left, right):
    return dot(left[0], right[0]) + dot(left[1], right[0]) + dot(left[0], right[1])


def crossed(value):
    top = jnp.concatenate([value[0:128, 0:128], value[128:256, 0:128]], 1)
    bottom = jnp.concatenate([value[0:128, 128:256], value[128:256, 128:256]], 1)
    return jnp.concatenate([top, bottom], 0)


def one_line(x, sens, cot, w):
    g_real = cot[0, pl.ds(x, 128, stride=8), :]
    g_imag = cot[1, pl.ds(x, 128, stride=8), :]
    s = [[sens[coil, part, pl.ds(x, 128, stride=8), :] for part in range(2)] for coil in range(2)]
    real = [s[k][0] * g_real - s[k][1] * g_imag for k in range(2)]
    imag = [s[k][0] * g_imag + s[k][1] * g_real for k in range(2)]
    value = jnp.concatenate([jnp.concatenate(real, 1), jnp.concatenate(imag, 1)], 0)
    forward = (w.tables[0], w.tables[1])
    backward = (w.tables[2], w.tables[3])
    value = crossed(product3(forward, split2(value)))
    value = product3(split2(value), backward)
    kept = w.mask[...].astype(F32)
    kept = jnp.concatenate([kept, kept], 1)
    value = value * jnp.concatenate([kept, kept], 0)
    value = crossed(product3(split2(value), forward))
    value = product3(backward, split2(value))
    real = [value[0:128, 128 * k : 128 * k + 128] for k in range(2)]
    imag = [value[128:256, 128 * k : 128 * k + 128] for k in range(2)]
    w.partial[x, 0] = sum(s[k][0] * real[k] + s[k][1] * imag[k] for k in range(2))
    w.partial[x, 1] = sum(s[k][0] * imag[k] - s[k][1] * real[k] for k in range(2))


class Refs:
    def __init__(self, **refs):
        self.__dict__.update(refs)


WEIGHTS = ("mask", "embed", "gain", "qkv", "proj", "unembed", "wide", "narrow", "tables")
WORK = dict(
    pad=((128, 384), F32),
    gain_col=((CHANNELS, 128), F32),
    to_embed=((GROUPS, CHANNELS, 192), BF16),
    to_mixed=((GROUPS, CHANNELS, 192), BF16),
    from_embed=((2, GROUPS, 32, CHANNELS), BF16),
    qkv_t=((384, 128), BF16),
    turn=((128, 128), F32),
    field=((WINDOWS, 2, 32, 128), F32),
    label=((WINDOWS, 8, 128), F32),
    unit=((CHANNELS, TOKENS), F32),
    mixed=((CHANNELS, TOKENS), F32),
    d_proj=((288, TOKENS), F32),
    d_field=((WINDOWS, 32, 128), F32),
    partial=((8, 2, 128, 128), F32),
)
SLABS = 16
COILS = 8
RING = 4


def kernel(image, cot, sens, labels, *rest):
    weights = rest[: len(WEIGHTS)]
    out = rest[len(WEIGHTS)]
    scratch = rest[len(WEIGHTS) + 1 :]
    w = Refs(**dict(zip(WEIGHTS, weights)), **dict(zip(WORK, scratch)))
    (col, lab, piece, sens_all, cot_all, coil_sum, swin_in, final, sems) = scratch[len(WORK) :]
    (own_sem, lab_sem, col_sem, cot1_sem, cot2_sem, sens_sem, sum_sem, swin_sem, out_sem, send_sem) = [
        sems.at[i] for i in range(10)
    ]
    s = lax.axis_index("slab")
    c = lax.axis_index("coil")
    xi = lax.rem(c, RING)
    sends = []

    def send(source, target, recv, device):
        copy = pltpu.make_async_remote_copy(
            src_ref=source, dst_ref=target, send_sem=send_sem, recv_sem=recv,
            device_id=device, device_id_type=MESH,
        )
        copy.start()
        sends.append(copy)

    def local(source, target, sem):
        pltpu.make_async_copy(source, target, sem).start()

    def await_bytes(ref, sem):
        pltpu.make_async_copy(ref, ref, sem).wait()

    def span(start, size, step):
        return pl.ds(pl.multiple_of(start, step), size)

    two = pl.ds(2 * xi, 2)
    for d in range(1, SLABS):
        t = lax.rem(s + d, SLABS)
        send(cot.at[:, two, span(8 * t, 8, 8), :], cot_all.at[:, s, xi], cot1_sem, {"slab": t})
    local(cot.at[:, two, span(8 * s, 8, 8), :], cot_all.at[:, s, xi], cot1_sem)
    below = lax.rem(s + SLABS - 1, SLABS)
    for arr, field in enumerate((image, cot)):
        for half in range(2):
            xs = span(lax.rem(16 * c + 8 + 8 * half, 128), 8, 8)
            place = slice(8 * half, 8 * half + 8)
            send(field.at[:, 0:4, xs, :], col.at[arr, :, 4:8, place, :], col_sem, {"slab": below})
            local(field.at[:, 4:8, xs, :], col.at[arr, :, 0:4, place, :], col_sem)
    local(labels.at[:, span(8 * c, 8, 8), :], lab, lab_sem)
    for coil in range(2):
        for d in range(1, SLABS):
            t = lax.rem(s + d, SLABS)
            send(
                sens.at[coil, :, :, span(8 * t, 8, 8), :],
                sens_all.at[coil, :, pl.ds(8 * s, 8)],
                sens_sem,
                {"slab": t},
            )
        local(
            sens.at[coil, :, :, span(8 * s, 8, 8), :], sens_all.at[coil, :, pl.ds(8 * s, 8)], sens_sem
        )
    prepare_weights(w)
    await_bytes(cot_all.at[:, :, 0], cot1_sem)
    for d in range(1, RING):
        t = c - xi + lax.rem(xi + d, RING)
        send(cot_all.at[:, :, xi], cot_all.at[:, :, xi], cot2_sem, {"coil": t})
    await_bytes(col, col_sem)
    await_bytes(lab, lab_sem)
    prepare_fields(col, lab, w)
    lax.fori_loop(0, WINDOWS, lambda win, carry: (one_window(win, w), carry)[1], 0)
    finish_fields(piece, w)

    conditional = []

    def send_or_copy(source, target, recv, slab, coil):
        mine = (slab == s) & (coil == c)
        copy = pltpu.make_async_remote_copy(
            src_ref=source, dst_ref=target, send_sem=send_sem, recv_sem=recv,
            device_id={"slab": slab, "coil": coil}, device_id_type=MESH,
        )

        @pl.when(mine)
        def _():
            local(source, target, recv)

        @pl.when(jnp.logical_not(mine))
        def _():
            copy.start()

        conditional.append((mine, copy))

    for half in range(2):
        to_slab = lax.rem(2 * c + 1 + half, SLABS)
        for upper in range(2):
            to_coil = lax.rem(s + upper, SLABS) // 2
            quarter = (1 + 2 * lax.rem(s, 2)) if not upper else (2 - 2 * lax.rem(s, 2))
            send_or_copy(
                piece.at[:, 4 * upper : 4 * upper + 4, 8 * half : 8 * half + 8, :],
                swin_in.at[:, pl.ds(4 * quarter, 4)],
                swin_sem,
                to_slab,
                to_coil,
            )

    await_bytes(sens_all, sens_sem)
    await_bytes(cot_all.at[:, :, 0:3], cot2_sem)
    sens_rows = sens_all.reshape(2, 2, 1024, 128)
    cot_rows = cot_all.reshape(2, 1024, 128)
    for x in range(8):
        one_line(x, sens_rows, cot_rows, w)
        if x % 4 == 3:
            xs = slice(x - 3, x + 1)
            for d in range(1, COILS):
                t = lax.rem(c + d, COILS)
                send(w.partial.at[xs, :, span(16 * t, 16, 16), :], coil_sum.at[d, xs], sum_sem, {"coil": t})
    await_bytes(coil_sum.at[1:8], sum_sem)
    await_bytes(swin_in, swin_sem)
    final_rows = final.reshape(2, 128, 128)
    for x in range(8):
        for part in range(2):
            total = w.partial[x, part, span(16 * c, 16, 16), :]
            for d in range(1, COILS):
                total = total + coil_sum[d, x, part]
            final_rows[part, pl.ds(x, 16, stride=8), :] = total * -STEP_SIZE
    mine16 = cot_all.reshape(2, 128, 8, 128)
    final[...] = final[...] + mine16[:, pl.ds(16 * c, 16)] + swin_in[...]
    for j in range(2):
        for d in range(COILS):
            t = lax.rem(c + d, COILS)
            source = final.at[:, 8 * j : 8 * j + 8]
            target = out.at[:, :, span(8 * s, 8, 8), :]
            if d:
                send(source, target, out_sem, {"slab": 2 * c + j, "coil": t})
            else:
                send_or_copy(source, target, out_sem, 2 * c + j, c)
    await_bytes(out, out_sem)
    for copy in sends:
        copy.wait_send()
    for mine, copy in conditional:
        @pl.when(jnp.logical_not(mine))
        def _(copy=copy):
            copy.wait_send()


def body(image, cotangent, sens, mask, labels, embed_weight, ln_gain, qkv_weight, proj_weight, unembed_weight):
    wide, narrow = selections()
    whole = pl.BlockSpec(memory_space=pltpu.VMEM)
    anywhere = pl.BlockSpec(memory_space=pl.ANY)
    scratch = [pltpu.VMEM(shape, dtype) for shape, dtype in WORK.values()]
    scratch += [
        pltpu.VMEM((2, 2, 8, 16, 128), F32),
        pltpu.VMEM((8, 8, 64), jnp.int32),
        pltpu.VMEM((2, 8, 16, 128), F32),
        pltpu.VMEM((2, 2, 128, 8, 128), F32),
        pltpu.VMEM((2, 16, 4, 2, 8, 128), F32),
        pltpu.VMEM((8, 8, 2, 16, 128), F32),
        pltpu.VMEM((2, 16, 8, 128), F32),
        pltpu.VMEM((2, 16, 8, 128), F32),
        pltpu.SemaphoreType.DMA((10,)),
    ]
    return pl.pallas_call(
        kernel,
        out_shape=jax.ShapeDtypeStruct(image.shape, F32),
        in_specs=[anywhere] * 4 + [whole] * len(WEIGHTS),
        out_specs=anywhere,
        scratch_shapes=scratch,
        compiler_params=pltpu.CompilerParams(has_side_effects=True, vmem_limit_bytes=48 * 1024 * 1024),
    )(
        image, cotangent, sens, labels, mask, embed_weight, ln_gain.reshape(1, CHANNELS), qkv_weight,
        proj_weight, unembed_weight, jnp.asarray(wide), jnp.asarray(narrow), jnp.asarray(dft_tables(128)),
    )


def solution(mesh):
    placed = (
        P(None, "slab", None, None),
        P(None, "slab", None, None),
        P("coil", None, "slab", None, None),
        P(),
        P("slab", None, None),
        P(),
        P(),
        P(),
        P(),
        P(),
    )
    return jax.shard_map(
        body, mesh=mesh, in_specs=placed, out_specs=P(None, "slab", None, None), check_vma=False
    )
```

```python
import functools

import jax
import jax.numpy as jnp
import numpy as np
from jax import lax
from jax.experimental import pallas as pl
from jax.experimental.pallas import tpu as pltpu
from jax.sharding import PartitionSpec as P

MESH = pl.DeviceIdType.MESH
F32 = jnp.float32
BF16 = jnp.bfloat16
HEADS = 3
HEAD = 32
CHANNELS = 96
WINDOWS = 8
TOKENS = 512
GROUPS = 4
CHUNK = 256
EPSILON = 1e-5
STEP_SIZE = 0.5
SCALE = HEAD ** -0.5
PENALTY = 1e9


def dft_tables(length):
    index = np.arange(length)
    angle = (index[:, None] * index[None, :] % length) * (2.0 * np.pi / length)
    cos = np.cos(angle) / np.sqrt(length)
    sin = np.sin(angle) / np.sqrt(length)
    forward = np.block([[cos, sin], [-sin, cos]])
    high = forward.astype(jnp.bfloat16)
    low = (forward - high.astype(np.float64)).astype(jnp.bfloat16)
    return np.stack([high, low, np.ascontiguousarray(high.T), np.ascontiguousarray(low.T)])


def selections():
    select = np.zeros((GROUPS, 8, 32), np.float32)
    for t in range(GROUPS):
        for f in range(8):
            part, px, py = f // 4, f // 2 % 2, f % 2
            select[t, f, part * 16 + px * 8 + 2 * t + py] = 1.0
    wide = np.zeros((3, GROUPS, 8, 192), np.float32)
    for slot, piece in enumerate((0, 0, 0, 1, 1, 2)):
        wide[piece, :, :, 32 * slot : 32 * slot + 32] = select
    return wide, np.ascontiguousarray(select.transpose(0, 2, 1))


def dot(left, right):
    return jnp.dot(left, right, preferred_element_type=F32)


def split2(value):
    high = value.astype(BF16)
    return high, (value - high.astype(F32)).astype(BF16)


def split3(value):
    high = value.astype(BF16)
    rest = value - high.astype(F32)
    middle = rest.astype(BF16)
    return high, middle, (rest - middle.astype(F32)).astype(BF16)


def lane_index(shape):
    return lax.broadcasted_iota(jnp.int32, shape, len(shape) - 1)


def prepare_weights(w):
    wide, narrow = w.wide, w.narrow
    emb = w.embed[...]
    w.pad[...] = jnp.zeros((128, 384), F32)
    w.pad[0:8, 0:CHANNELS] = emb
    w.pad[8:16, 0:CHANNELS] = jnp.broadcast_to(w.gain[...], (8, CHANNELS))
    w.pad[16:24, 0:CHANNELS] = w.unembed[...]
    turned = jnp.transpose(w.pad[:, 0:128])
    w.gain_col[...] = jnp.broadcast_to(turned[0:CHANNELS, 8:9], (CHANNELS, 128))
    emb_t = split3(turned[0:CHANNELS, 0:8])
    un = split3(turned[0:CHANNELS, 16:24])
    emb_pieces = split2(emb)
    for t in range(GROUPS):
        w.to_embed[t] = sum(dot(p.astype(F32), wide[i, t]) for i, p in enumerate(emb_t)).astype(BF16)
        w.to_mixed[t] = sum(dot(p.astype(F32), wide[i, t]) for i, p in enumerate(un)).astype(BF16)
        for i, p in enumerate(emb_pieces):
            w.from_embed[i, t] = dot(narrow[t], p.astype(F32)).astype(BF16)
    w.pad[0:CHANNELS, 0:288] = w.qkv[...].astype(F32)
    for b in range(3):
        w.qkv_t[128 * b : 128 * b + 128, :] = jnp.transpose(w.pad[:, 128 * b : 128 * b + 128]).astype(BF16)


def prepare_fields(col, lab, w):
    rows = col.reshape(2, 2, 128, 128)
    low = lane_index((8, 128)) < 64
    for part in range(2):
        for px in range(2):
            both = jnp.concatenate(
                [rows[arr, part, pl.ds(px, 64, stride=2), :] for arr in range(2)], 0
            )
            w.turn[...] = jnp.transpose(both)
            place = 8 * (part * 2 + px)
            for win in range(WINDOWS):
                first = w.turn[8 * ((2 * win + 1) % 16) : 8 * ((2 * win + 1) % 16) + 8, :]
                second = w.turn[8 * ((2 * win + 2) % 16) : 8 * ((2 * win + 2) % 16) + 8, :]
                w.field[win, 0, place : place + 8, :] = jnp.where(low, first, pltpu.roll(second, 64, 1))
                w.field[win, 1, place : place + 8, :] = jnp.where(low, pltpu.roll(first, 64, 1), second)
    w.pad[:, 0:128] = jnp.zeros((128, 128), F32)
    for z in range(8):
        w.pad[8 * z : 8 * z + 8, 0:64] = lab[z].astype(F32)
    w.turn[...] = jnp.transpose(w.pad[:, 0:128])
    for win in range(WINDOWS):
        tile = w.turn[8 * win : 8 * win + 8, :]
        moved = pltpu.roll(pltpu.roll(tile, 4, 0), 64, 1)
        w.label[win] = jnp.where(low, tile, moved)


def one_window(win, w):
    image6 = split3(w.field[win, 0])
    grad6 = split3(w.field[win, 1])
    order = (0, 1, 2, 0, 1, 0)
    image6 = jnp.concatenate([image6[i] for i in order], 0)
    grad6 = jnp.concatenate([grad6[i] for i in order], 0)
    embedded = jnp.concatenate([dot(w.to_embed[t], image6) for t in range(GROUPS)], 1)
    mixed = jnp.concatenate([dot(w.to_mixed[t], grad6) for t in range(GROUPS)], 1)
    label = w.label[win]
    label = jnp.concatenate([label[t : t + 1, :] for t in range(GROUPS)], 1)

    gain = jnp.concatenate([w.gain_col[...]] * GROUPS, 1)
    mean = jnp.sum(embedded, 0, keepdims=True) * (1.0 / CHANNELS)
    centered = embedded - mean
    variance = jnp.sum(centered * centered, 0, keepdims=True) * (1.0 / CHANNELS)
    inverse = lax.rsqrt(variance + EPSILON)
    unit = centered * inverse
    w.unit[...] = unit
    normed = (unit * gain).astype(BF16)
    projected = dot(w.qkv_t[0:288, :][:, 0:CHANNELS], normed).astype(BF16).astype(F32)
    proj = w.proj[...]
    mixed_high, mixed_low = split2(mixed)
    attended = (dot(proj, mixed_high) + dot(proj, mixed_low)).astype(BF16).astype(F32)
    w.mixed[...] = mixed

    row = lax.broadcasted_iota(jnp.int32, (HEAD, TOKENS), 0)
    zero_f = jnp.zeros((HEAD, TOKENS), F32)
    zero = zero_f.astype(BF16)
    label_key = jnp.where(row == 0, label, jnp.where(row == 1, 1.0 - label, 0.0))
    label_query = jnp.where(row == 0, label - 1.0, jnp.where(row == 1, -label, 0.0)) * PENALTY
    label_query = label_query.astype(BF16)
    lane = lane_index((1, 128))
    only_query = ((lane >= 64) & (lane < 96)).astype(F32)
    only_grad = (lane >= 96).astype(F32)
    lane_scale = jnp.where(lane < 96, SCALE, 1.0).astype(F32)

    for head in range(HEADS):
        at = HEAD * head
        query = projected[at : at + HEAD]
        key = projected[CHANNELS + at : CHANNELS + at + HEAD]
        value = projected[2 * CHANNELS + at : 2 * CHANNELS + at + HEAD]
        grad = attended[at : at + HEAD]
        token = jnp.transpose(jnp.concatenate([key, value, query, grad], 0))
        more = jnp.transpose(jnp.concatenate([key, key, label_key, zero_f], 0))
        token_query = (token * only_query).astype(BF16)
        token_grad = (token * only_grad).astype(BF16)
        token = token.astype(BF16)
        left = jnp.concatenate([token, more.astype(BF16)], 1)
        parts = split3(query * (SCALE * float(np.log2(np.e))))
        right = jnp.concatenate(
            [parts[0], zero, zero, zero, parts[1], parts[2], label_query, zero], 0
        )
        right_value = jnp.concatenate([zero, grad.astype(BF16), zero, zero], 0)
        key16 = key.astype(BF16)
        total = jnp.zeros((TOKENS, 128), F32)
        for chunk in range(TOKENS // CHUNK):
            cut = slice(CHUNK * chunk, CHUNK * chunk + CHUNK)
            scores = dot(left, right[:, cut])
            top = jnp.max(scores, 0, keepdims=True)
            weights = jnp.exp2(scores - top)
            soft = weights * (1.0 / jnp.sum(weights, 0, keepdims=True))
            d_soft = dot(token, right_value[:, cut]).astype(BF16).astype(F32)
            inner = jnp.sum(d_soft * soft, 0, keepdims=True)
            d_scores = (soft * (d_soft - inner)).astype(BF16)
            w.d_proj[at : at + HEAD, cut] = dot(key16, d_scores) * SCALE
            total = total + dot(soft.astype(BF16), token_grad[cut, :]) + dot(d_scores, token_query[cut, :])
        total = jnp.transpose(total * lane_scale)
        w.d_proj[CHANNELS + at : CHANNELS + at + HEAD, :] = total[64:96]
        w.d_proj[2 * CHANNELS + at : 2 * CHANNELS + at + HEAD, :] = total[96:128]

    d_normed = dot(w.qkv[...], w.d_proj[...].astype(BF16)).astype(BF16).astype(F32)
    d_unit = d_normed * gain
    unit = w.unit[...]
    first = jnp.sum(d_unit, 0, keepdims=True) * (1.0 / CHANNELS)
    second = jnp.sum(d_unit * unit, 0, keepdims=True) * (1.0 / CHANNELS)
    d_embedded = inverse * (d_unit - first - unit * second) + w.mixed[...]
    high, low = split2(d_embedded)
    result = jnp.zeros((32, 128), F32)
    for t in range(GROUPS):
        cut = slice(128 * t, 128 * t + 128)
        result += dot(w.from_embed[0, t], high[:, cut])
        result += dot(w.from_embed[0, t], low[:, cut])
        result += dot(w.from_embed[1, t], high[:, cut])
    w.d_field[win] = result


def finish_fields(piece, w):
    rows = piece.reshape(2, 128, 128)
    low = lane_index((8, 128)) < 64
    for px in range(2):
        for win in range(WINDOWS):
            real = w.d_field[win, 8 * px : 8 * px + 8, :]
            imag = w.d_field[win, 16 + 8 * px : 24 + 8 * px, :]
            first = 8 * ((2 * win + 1) % 16)
            second = 8 * ((2 * win + 2) % 16)
            w.turn[first : first + 8, :] = jnp.where(low, real, pltpu.roll(imag, 64, 1))
            w.turn[second : second + 8, :] = jnp.where(low, pltpu.roll(real, 64, 1), imag)
        turned = jnp.transpose(w.turn[...])
        for part in range(2):
            rows[part, pl.ds(px, 64, stride=2), :] = turned[64 * part : 64 * part + 64, :]


def product3(left, right):
    return dot(left[0], right[0]) + dot(left[1], right[0]) + dot(left[0], right[1])


def crossed(value):
    top = jnp.concatenate([value[0:128, 0:128], value[128:256, 0:128]], 1)
    bottom = jnp.concatenate([value[0:128, 128:256], value[128:256, 128:256]], 1)
    return jnp.concatenate([top, bottom], 0)


def one_line(x, sens, cot, w):
    g_real = cot[0, pl.ds(x, 128, stride=8), :]
    g_imag = cot[1, pl.ds(x, 128, stride=8), :]
    s = [[sens[coil, part, pl.ds(x, 128, stride=8), :] for part in range(2)] for coil in range(2)]
    real = [s[k][0] * g_real - s[k][1] * g_imag for k in range(2)]
    imag = [s[k][0] * g_imag + s[k][1] * g_real for k in range(2)]
    value = jnp.concatenate([jnp.concatenate(real, 1), jnp.concatenate(imag, 1)], 0)
    forward = (w.tables[0], w.tables[1])
    backward = (w.tables[2], w.tables[3])
    value = crossed(product3(forward, split2(value)))
    value = product3(split2(value), backward)
    kept = w.mask[...].astype(F32)
    kept = jnp.concatenate([kept, kept], 1)
    value = value * jnp.concatenate([kept, kept], 0)
    value = crossed(product3(split2(value), forward))
    value = product3(backward, split2(value))
    real = [value[0:128, 128 * k : 128 * k + 128] for k in range(2)]
    imag = [value[128:256, 128 * k : 128 * k + 128] for k in range(2)]
    w.partial[x, 0] = sum(s[k][0] * real[k] + s[k][1] * imag[k] for k in range(2))
    w.partial[x, 1] = sum(s[k][0] * imag[k] - s[k][1] * real[k] for k in range(2))


class Refs:
    def __init__(self, **refs):
        self.__dict__.update(refs)


WEIGHTS = dict(
    mask=((128, 128), jnp.int32),
    embed=((8, CHANNELS), F32),
    gain=((1, CHANNELS), F32),
    qkv=((CHANNELS, 288), BF16),
    proj=((CHANNELS, CHANNELS), BF16),
    unembed=((8, CHANNELS), F32),
    wide=((3, GROUPS, 8, 192), F32),
    narrow=((GROUPS, 32, 8), F32),
    tables=((4, 256, 256), BF16),
)
WORK = dict(
    pad=((128, 384), F32),
    gain_col=((CHANNELS, 128), F32),
    to_embed=((GROUPS, CHANNELS, 192), BF16),
    to_mixed=((GROUPS, CHANNELS, 192), BF16),
    from_embed=((2, GROUPS, 32, CHANNELS), BF16),
    qkv_t=((384, 128), BF16),
    turn=((128, 128), F32),
    field=((WINDOWS, 2, 32, 128), F32),
    label=((WINDOWS, 8, 128), F32),
    unit=((CHANNELS, TOKENS), F32),
    mixed=((CHANNELS, TOKENS), F32),
    d_proj=((288, TOKENS), F32),
    d_field=((WINDOWS, 32, 128), F32),
    partial=((8, 2, 128, 128), F32),
)
EARLY = 5
VMEM_LIMIT = 60 * 1024 * 1024
SLABS = 16
COILS = 8
RING = 4


def kernel(image, cot, sens, labels, *rest):
    weights = rest[: len(WEIGHTS)]
    out = rest[len(WEIGHTS)]
    held = rest[len(WEIGHTS) + 1 : 2 * len(WEIGHTS) + 1]
    scratch = rest[2 * len(WEIGHTS) + 1 :]
    w = Refs(**dict(zip(WEIGHTS, held)), **dict(zip(WORK, scratch)))
    (col, lab, piece, sens_all, cot_all, coil_sum, swin_in, final, sems, ready) = scratch[len(WORK) :]
    (own_sem, lab_sem, col_sem, cot1_sem, cot2_sem, sens_sem, sum_sem, swin_sem, out_sem, send_sem) = [
        sems.at[i] for i in range(10)
    ]
    s = lax.axis_index("slab")
    c = lax.axis_index("coil")
    xi = lax.rem(c, RING)
    sends = []

    def send(source, target, recv, device):
        copy = pltpu.make_async_remote_copy(
            src_ref=source, dst_ref=target, send_sem=send_sem, recv_sem=recv,
            device_id=device, device_id_type=MESH,
        )
        copy.start()
        sends.append(copy)

    def local(source, target, sem):
        pltpu.make_async_copy(source, target, sem).start()

    def await_bytes(ref, sem):
        pltpu.make_async_copy(ref, ref, sem).wait()

    def span(start, size, step):
        return pl.ds(pl.multiple_of(start, step), size)

    barrier = pltpu.get_barrier_semaphore()
    for d in range(1, SLABS):
        pl.semaphore_signal(barrier, inc=1, device_id={"slab": lax.rem(s + d, SLABS)}, device_id_type=MESH)
    for d in range(1, COILS):
        pl.semaphore_signal(barrier, inc=1, device_id={"coil": lax.rem(c + d, COILS)}, device_id_type=MESH)
    for source, target in zip(weights, held):
        local(source, target, own_sem)
    local(labels.at[:, span(8 * c, 8, 8), :], lab, lab_sem)
    pl.semaphore_wait(barrier, SLABS + COILS - 2)
    def windows(first, last):
        lax.fori_loop(first, last, lambda win, carry: (one_window(win, w), carry)[1], 0)

    two = pl.ds(2 * xi, 2)
    for d in range(1, SLABS):
        t = lax.rem(s + d, SLABS)
        send(cot.at[:, two, span(8 * t, 8, 8), :], cot_all.at[:, s, xi], cot1_sem, {"slab": t})
    local(cot.at[:, two, span(8 * s, 8, 8), :], cot_all.at[:, s, xi], cot1_sem)
    below = lax.rem(s + SLABS - 1, SLABS)
    for arr, field in enumerate((image, cot)):
        for half in range(2):
            xs = span(lax.rem(16 * c + 8 + 8 * half, 128), 8, 8)
            place = slice(8 * half, 8 * half + 8)
            send(field.at[:, 0:4, xs, :], col.at[arr, :, 4:8, place, :], col_sem, {"slab": below})
            local(field.at[:, 4:8, xs, :], col.at[arr, :, 0:4, place, :], col_sem)
    for coil in range(2):
        for d in range(1, SLABS):
            t = lax.rem(s + d, SLABS)
            send(
                sens.at[coil, :, :, span(8 * t, 8, 8), :],
                sens_all.at[coil, :, pl.ds(8 * s, 8)],
                sens_sem,
                {"slab": t},
            )
        local(
            sens.at[coil, :, :, span(8 * s, 8, 8), :], sens_all.at[coil, :, pl.ds(8 * s, 8)], sens_sem
        )
    for d in range(1, SLABS):
        pl.semaphore_signal(ready, inc=1, device_id={"slab": lax.rem(s + d, SLABS)}, device_id_type=MESH)
    for target in held:
        await_bytes(target, own_sem)
    prepare_weights(w)
    await_bytes(cot_all.at[:, :, 0], cot1_sem)
    for d in range(1, RING):
        t = c - xi + lax.rem(xi + d, RING)
        send(cot_all.at[:, :, xi], cot_all.at[:, :, xi], cot2_sem, {"coil": t})
    await_bytes(col, col_sem)
    await_bytes(lab, lab_sem)
    prepare_fields(col, lab, w)
    windows(0, EARLY)
    await_bytes(sens_all, sens_sem)
    await_bytes(cot_all.at[:, :, 0:3], cot2_sem)
    sens_rows = sens_all.reshape(2, 2, 1024, 128)
    cot_rows = cot_all.reshape(2, 1024, 128)
    for x in range(8):
        one_line(x, sens_rows, cot_rows, w)
        if x % 4 == 3:
            xs = slice(x - 3, x + 1)
            for d in range(1, COILS):
                t = lax.rem(c + d, COILS)
                send(w.partial.at[xs, :, span(16 * t, 16, 16), :], coil_sum.at[d, xs], sum_sem, {"coil": t})
    windows(EARLY, WINDOWS)
    finish_fields(piece, w)
    pl.semaphore_wait(ready, SLABS - 1)
    conditional = []

    def send_or_copy(source, target, recv, slab, coil):
        mine = (slab == s) & (coil == c)
        copy = pltpu.make_async_remote_copy(
            src_ref=source, dst_ref=target, send_sem=send_sem, recv_sem=recv,
            device_id={"slab": slab, "coil": coil}, device_id_type=MESH,
        )

        @pl.when(mine)
        def _():
            local(source, target, recv)

        @pl.when(jnp.logical_not(mine))
        def _():
            copy.start()

        conditional.append((mine, copy))

    for half in range(2):
        to_slab = lax.rem(2 * c + 1 + half, SLABS)
        for upper in range(2):
            to_coil = lax.rem(s + upper, SLABS) // 2
            quarter = (1 + 2 * lax.rem(s, 2)) if not upper else (2 - 2 * lax.rem(s, 2))
            send_or_copy(
                piece.at[:, 4 * upper : 4 * upper + 4, 8 * half : 8 * half + 8, :],
                swin_in.at[:, pl.ds(4 * quarter, 4)],
                swin_sem,
                to_slab,
                to_coil,
            )

    await_bytes(coil_sum.at[1:8], sum_sem)
    await_bytes(swin_in, swin_sem)
    final_rows = final.reshape(2, 128, 128)
    for x in range(8):
        for part in range(2):
            total = w.partial[x, part, span(16 * c, 16, 16), :]
            for d in range(1, COILS):
                total = total + coil_sum[d, x, part]
            final_rows[part, pl.ds(x, 16, stride=8), :] = total * -STEP_SIZE
    mine16 = cot_all.reshape(2, 128, 8, 128)
    final[...] = final[...] + mine16[:, pl.ds(16 * c, 16)] + swin_in[...]
    for j in range(2):
        for d in range(COILS):
            t = lax.rem(c + d, COILS)
            source = final.at[:, 8 * j : 8 * j + 8]
            target = out.at[:, :, span(8 * s, 8, 8), :]
            if d:
                send(source, target, out_sem, {"slab": 2 * c + j, "coil": t})
            else:
                send_or_copy(source, target, out_sem, 2 * c + j, c)
    await_bytes(out, out_sem)
    for copy in sends:
        copy.wait_send()
    for mine, copy in conditional:
        @pl.when(jnp.logical_not(mine))
        def _(copy=copy):
            copy.wait_send()


def body(image, cotangent, sens, mask, labels, embed_weight, ln_gain, qkv_weight, proj_weight, unembed_weight):
    wide, narrow = selections()
    anywhere = pl.BlockSpec(memory_space=pl.ANY)
    scratch = [pltpu.VMEM(shape, dtype) for held in (WEIGHTS, WORK) for shape, dtype in held.values()]
    scratch += [
        pltpu.VMEM((2, 2, 8, 16, 128), F32),
        pltpu.VMEM((8, 8, 64), jnp.int32),
        pltpu.VMEM((2, 8, 16, 128), F32),
        pltpu.VMEM((2, 2, 128, 8, 128), F32),
        pltpu.VMEM((2, 16, 4, 2, 8, 128), F32),
        pltpu.VMEM((8, 8, 2, 16, 128), F32),
        pltpu.VMEM((2, 16, 8, 128), F32),
        pltpu.VMEM((2, 16, 8, 128), F32),
        pltpu.SemaphoreType.DMA((10,)),
        pltpu.SemaphoreType.REGULAR,
    ]
    return pl.pallas_call(
        kernel,
        out_shape=jax.ShapeDtypeStruct(image.shape, F32),
        in_specs=[anywhere] * (4 + len(WEIGHTS)),
        out_specs=anywhere,
        scratch_shapes=scratch,
        compiler_params=pltpu.CompilerParams(
            collective_id=0, has_side_effects=True, vmem_limit_bytes=VMEM_LIMIT
        ),
    )(
        image, cotangent, sens, labels, mask, embed_weight, ln_gain.reshape(1, CHANNELS), qkv_weight,
        proj_weight, unembed_weight.T, jnp.asarray(wide), jnp.asarray(narrow), jnp.asarray(dft_tables(128)),
    )


def solution(mesh):
    placed = (
        P(None, "slab", None, None),
        P(None, "slab", None, None),
        P("coil", None, "slab", None, None),
        P(),
        P("slab", None, None),
        P(),
        P(),
        P(),
        P(),
        P(),
    )
    return jax.shard_map(
        body, mesh=mesh, in_specs=placed, out_specs=P(None, "slab", None, None), check_vma=False
    )
```

```python
import functools

import jax
import jax.numpy as jnp
import numpy as np
from jax import lax
from jax.experimental import pallas as pl
from jax.experimental.pallas import tpu as pltpu
from jax.sharding import PartitionSpec as P

MESH = pl.DeviceIdType.MESH
F32 = jnp.float32
BF16 = jnp.bfloat16
HEADS = 3
HEAD = 32
CHANNELS = 96
WINDOWS = 8
TOKENS = 512
GROUPS = 4
CHUNK = 256
EPSILON = 1e-5
STEP_SIZE = 0.5
SCALE = HEAD ** -0.5
PENALTY = 1e9


def dft_tables(length):
    index = np.arange(length)
    angle = (index[:, None] * index[None, :] % length) * (2.0 * np.pi / length)
    cos = np.cos(angle) / np.sqrt(length)
    sin = np.sin(angle) / np.sqrt(length)
    forward = np.block([[cos, sin], [-sin, cos]])
    high = forward.astype(jnp.bfloat16)
    low = (forward - high.astype(np.float64)).astype(jnp.bfloat16)
    return np.stack([high, low, np.ascontiguousarray(high.T), np.ascontiguousarray(low.T)])


def selections():
    select = np.zeros((GROUPS, 8, 32), np.float32)
    for t in range(GROUPS):
        for f in range(8):
            part, px, py = f // 4, f // 2 % 2, f % 2
            select[t, f, part * 16 + px * 8 + 2 * t + py] = 1.0
    wide = np.zeros((3, GROUPS, 8, 192), np.float32)
    for slot, piece in enumerate((0, 0, 0, 1, 1, 2)):
        wide[piece, :, :, 32 * slot : 32 * slot + 32] = select
    return wide, np.ascontiguousarray(select.transpose(0, 2, 1))


def dot(left, right):
    return jnp.dot(left, right, preferred_element_type=F32)


def split2(value):
    high = value.astype(BF16)
    return high, (value - high.astype(F32)).astype(BF16)


def split3(value):
    high = value.astype(BF16)
    rest = value - high.astype(F32)
    middle = rest.astype(BF16)
    return high, middle, (rest - middle.astype(F32)).astype(BF16)


def lane_index(shape):
    return lax.broadcasted_iota(jnp.int32, shape, len(shape) - 1)


def prepare_weights(w):
    wide, narrow = w.wide, w.narrow
    emb = w.embed[...]
    w.pad[...] = jnp.zeros((128, 384), F32)
    w.pad[0:8, 0:CHANNELS] = emb
    w.pad[8:16, 0:CHANNELS] = jnp.broadcast_to(w.gain[...], (8, CHANNELS))
    w.pad[16:24, 0:CHANNELS] = w.unembed[...]
    turned = jnp.transpose(w.pad[:, 0:128])
    w.gain_col[...] = jnp.broadcast_to(turned[0:CHANNELS, 8:9], (CHANNELS, 128))
    emb_t = split3(turned[0:CHANNELS, 0:8])
    un = split3(turned[0:CHANNELS, 16:24])
    emb_pieces = split2(emb)
    for t in range(GROUPS):
        w.to_embed[t] = sum(dot(p.astype(F32), wide[i, t]) for i, p in enumerate(emb_t)).astype(BF16)
        w.to_mixed[t] = sum(dot(p.astype(F32), wide[i, t]) for i, p in enumerate(un)).astype(BF16)
        for i, p in enumerate(emb_pieces):
            w.from_embed[i, t] = dot(narrow[t], p.astype(F32)).astype(BF16)
    w.pad[0:CHANNELS, 0:288] = w.qkv[...].astype(F32)
    for b in range(3):
        w.qkv_t[128 * b : 128 * b + 128, :] = jnp.transpose(w.pad[:, 128 * b : 128 * b + 128]).astype(BF16)


def prepare_fields(col, lab, w):
    rows = col.reshape(2, 2, 128, 128)
    low = lane_index((8, 128)) < 64
    for part in range(2):
        for px in range(2):
            both = jnp.concatenate(
                [rows[arr, part, pl.ds(px, 64, stride=2), :] for arr in range(2)], 0
            )
            w.turn[...] = jnp.transpose(both)
            place = 8 * (part * 2 + px)
            for win in range(WINDOWS):
                first = w.turn[8 * ((2 * win + 1) % 16) : 8 * ((2 * win + 1) % 16) + 8, :]
                second = w.turn[8 * ((2 * win + 2) % 16) : 8 * ((2 * win + 2) % 16) + 8, :]
                w.field[win, 0, place : place + 8, :] = jnp.where(low, first, pltpu.roll(second, 64, 1))
                w.field[win, 1, place : place + 8, :] = jnp.where(low, pltpu.roll(first, 64, 1), second)
    w.pad[:, 0:128] = jnp.zeros((128, 128), F32)
    for z in range(8):
        w.pad[8 * z : 8 * z + 8, 0:64] = lab[z].astype(F32)
    w.turn[...] = jnp.transpose(w.pad[:, 0:128])
    for win in range(WINDOWS):
        tile = w.turn[8 * win : 8 * win + 8, :]
        moved = pltpu.roll(pltpu.roll(tile, 4, 0), 64, 1)
        w.label[win] = jnp.where(low, tile, moved)


def one_window(win, w, beside=None):
    image6 = split3(w.field[win, 0])
    grad6 = split3(w.field[win, 1])
    order = (0, 1, 2, 0, 1, 0)
    image6 = jnp.concatenate([image6[i] for i in order], 0)
    grad6 = jnp.concatenate([grad6[i] for i in order], 0)
    embedded = jnp.concatenate([dot(w.to_embed[t], image6) for t in range(GROUPS)], 1)
    mixed = jnp.concatenate([dot(w.to_mixed[t], grad6) for t in range(GROUPS)], 1)
    label = w.label[win]
    label = jnp.concatenate([label[t : t + 1, :] for t in range(GROUPS)], 1)

    gain = jnp.concatenate([w.gain_col[...]] * GROUPS, 1)
    mean = jnp.sum(embedded, 0, keepdims=True) * (1.0 / CHANNELS)
    centered = embedded - mean
    variance = jnp.sum(centered * centered, 0, keepdims=True) * (1.0 / CHANNELS)
    inverse = lax.rsqrt(variance + EPSILON)
    unit = centered * inverse
    w.unit[...] = unit
    normed = (unit * gain).astype(BF16)
    projected = dot(w.qkv_t[0:288, :][:, 0:CHANNELS], normed).astype(BF16).astype(F32)
    proj = w.proj[...]
    mixed_high, mixed_low = split2(mixed)
    attended = (dot(proj, mixed_high) + dot(proj, mixed_low)).astype(BF16).astype(F32)
    w.mixed[...] = mixed

    row = lax.broadcasted_iota(jnp.int32, (HEAD, TOKENS), 0)
    zero_f = jnp.zeros((HEAD, TOKENS), F32)
    zero = zero_f.astype(BF16)
    label_key = jnp.where(row == 0, label, jnp.where(row == 1, 1.0 - label, 0.0))
    label_query = jnp.where(row == 0, label - 1.0, jnp.where(row == 1, -label, 0.0)) * PENALTY
    label_query = label_query.astype(BF16)
    lane = lane_index((1, 128))
    only_query = ((lane >= 64) & (lane < 96)).astype(F32)
    only_grad = (lane >= 96).astype(F32)
    lane_scale = jnp.where(lane < 96, SCALE, 1.0).astype(F32)

    def head_operands(head):
        at = HEAD * head
        query = projected[at : at + HEAD]
        key = projected[CHANNELS + at : CHANNELS + at + HEAD]
        value = projected[2 * CHANNELS + at : 2 * CHANNELS + at + HEAD]
        grad = attended[at : at + HEAD]
        token = jnp.transpose(jnp.concatenate([key, value, query, grad], 0))
        more = jnp.transpose(jnp.concatenate([key, key, label_key, zero_f], 0))
        token_query = (token * only_query).astype(BF16)
        token_grad = (token * only_grad).astype(BF16)
        token = token.astype(BF16)
        left = jnp.concatenate([token, more.astype(BF16)], 1)
        parts = split3(query * (SCALE * float(np.log2(np.e))))
        right = jnp.concatenate(
            [parts[0], zero, zero, zero, parts[1], parts[2], label_query, zero], 0
        )
        right_value = jnp.concatenate([zero, grad.astype(BF16), zero, zero], 0)
        return left, right, token, right_value, key.astype(BF16), token_grad, token_query

    def products(operands, chunk):
        left, right, token, right_value = operands[:4]
        cut = slice(CHUNK * chunk, CHUNK * chunk + CHUNK)
        scores = dot(left, right[:, cut])
        return scores, dot(token, right_value[:, cut]).astype(BF16)

    chunks = TOKENS // CHUNK
    steps = [(head, chunk) for head in range(HEADS) for chunk in range(chunks)]
    operands = {0: head_operands(0)}
    ahead = [products(operands[0], 0)]
    for index, (head, chunk) in enumerate(steps):
        at = HEAD * head
        cut = slice(CHUNK * chunk, CHUNK * chunk + CHUNK)
        scores, d_soft = ahead.pop(0)
        if beside is not None:
            beside(index)
        if index + 1 < len(steps):
            after, after_chunk = steps[index + 1]
            if after not in operands:
                operands[after] = head_operands(after)
            ahead.append(products(operands[after], after_chunk))
        key16, token_grad, token_query = operands[head][4:]
        top = jnp.max(scores, 0, keepdims=True)
        weights = jnp.exp2(scores - top)
        soft = weights * (1.0 / jnp.sum(weights, 0, keepdims=True))
        d_soft = d_soft.astype(F32)
        inner = jnp.sum(d_soft * soft, 0, keepdims=True)
        d_scores = (soft * (d_soft - inner)).astype(BF16)
        w.d_proj[at : at + HEAD, cut] = dot(key16, d_scores) * SCALE
        part = dot(soft.astype(BF16), token_grad[cut, :]) + dot(d_scores, token_query[cut, :])
        total = part if chunk == 0 else total + part
        if chunk == chunks - 1:
            turned = jnp.transpose(total * lane_scale)
            w.d_proj[CHANNELS + at : CHANNELS + at + HEAD, :] = turned[64:96]
            w.d_proj[2 * CHANNELS + at : 2 * CHANNELS + at + HEAD, :] = turned[96:128]

    d_normed = dot(w.qkv[...], w.d_proj[...].astype(BF16)).astype(BF16).astype(F32)
    d_unit = d_normed * gain
    unit = w.unit[...]
    first = jnp.sum(d_unit, 0, keepdims=True) * (1.0 / CHANNELS)
    second = jnp.sum(d_unit * unit, 0, keepdims=True) * (1.0 / CHANNELS)
    d_embedded = inverse * (d_unit - first - unit * second) + w.mixed[...]
    high, low = split2(d_embedded)
    result = jnp.zeros((32, 128), F32)
    for t in range(GROUPS):
        cut = slice(128 * t, 128 * t + 128)
        result += dot(w.from_embed[0, t], high[:, cut])
        result += dot(w.from_embed[0, t], low[:, cut])
        result += dot(w.from_embed[1, t], high[:, cut])
    w.d_field[win] = result


def finish_fields(piece, w):
    rows = piece.reshape(2, 128, 128)
    low = lane_index((8, 128)) < 64
    for px in range(2):
        for win in range(WINDOWS):
            real = w.d_field[win, 8 * px : 8 * px + 8, :]
            imag = w.d_field[win, 16 + 8 * px : 24 + 8 * px, :]
            first = 8 * ((2 * win + 1) % 16)
            second = 8 * ((2 * win + 2) % 16)
            w.turn[first : first + 8, :] = jnp.where(low, real, pltpu.roll(imag, 64, 1))
            w.turn[second : second + 8, :] = jnp.where(low, pltpu.roll(real, 64, 1), imag)
        turned = jnp.transpose(w.turn[...])
        for part in range(2):
            rows[part, pl.ds(px, 64, stride=2), :] = turned[64 * part : 64 * part + 64, :]


def product3(left, right):
    return dot(left[0], right[0]) + dot(left[1], right[0]) + dot(left[0], right[1])


def turned(value, count):
    blocks = []
    for coil in range(count):
        rows = slice(128 * coil, 128 * coil + 128)
        blocks.append(
            jnp.concatenate([jnp.transpose(value[rows, 0:128]), jnp.transpose(value[rows, 128:256])], 1)
        )
    return jnp.concatenate(blocks, 0)


def some_coils(sens, cot, w):
    coils = [sens[group, k] for group in range(sens.shape[0]) for k in range(2)]
    count = len(coils)
    g_real, g_imag = cot[0], cot[1]
    real = jnp.concatenate([s[0] * g_real - s[1] * g_imag for s in coils], 0)
    imag = jnp.concatenate([s[0] * g_imag + s[1] * g_real for s in coils], 0)
    forward = (w.tables[2], w.tables[3])
    backward = (w.tables[0], w.tables[1])
    value = turned(product3(split2(jnp.concatenate([real, imag], 1)), forward), count)
    value = product3(split2(value), forward)
    kept = jnp.concatenate([w.kept[...]] * count, 0)
    value = value * jnp.concatenate([kept, kept], 1)
    value = turned(product3(split2(value), backward), count)
    value = product3(split2(value), backward)
    real = sum(
        s[0] * value[128 * k : 128 * k + 128, 0:128] + s[1] * value[128 * k : 128 * k + 128, 128:256]
        for k, s in enumerate(coils)
    )
    imag = sum(
        s[0] * value[128 * k : 128 * k + 128, 128:256] - s[1] * value[128 * k : 128 * k + 128, 0:128]
        for k, s in enumerate(coils)
    )
    return real, imag


class Refs:
    def __init__(self, **refs):
        self.__dict__.update(refs)


WEIGHTS = dict(
    mask=((128, 128), jnp.int32),
    embed=((8, CHANNELS), F32),
    gain=((1, CHANNELS), F32),
    qkv=((CHANNELS, 288), BF16),
    proj=((CHANNELS, CHANNELS), BF16),
    unembed=((8, CHANNELS), F32),
    wide=((3, GROUPS, 8, 192), F32),
    narrow=((GROUPS, 32, 8), F32),
    tables=((4, 256, 256), BF16),
)
WORK = dict(
    pad=((128, 384), F32),
    gain_col=((CHANNELS, 128), F32),
    to_embed=((GROUPS, CHANNELS, 192), BF16),
    to_mixed=((GROUPS, CHANNELS, 192), BF16),
    from_embed=((2, GROUPS, 32, CHANNELS), BF16),
    qkv_t=((384, 128), BF16),
    turn=((128, 128), F32),
    field=((WINDOWS, 2, 32, 128), F32),
    label=((WINDOWS, 8, 128), F32),
    unit=((CHANNELS, TOKENS), F32),
    mixed=((CHANNELS, TOKENS), F32),
    d_proj=((288, TOKENS), F32),
    d_field=((WINDOWS, 32, 128), F32),
    kept=((128, 128), F32),
    line=((2, 128, 128), F32),
)
BUFFERS = (
    ((2, 2, 8, 16, 128), F32),
    ((8, 8, 64), jnp.int32),
    ((2, 8, 16, 128), F32),
    ((8, 2, 2, 128, 128), F32),
    ((2, 8, 16, 128), F32),
    ((2, 128, 128), F32),
    ((16, 2, 8, 128), F32),
    ((2, 4, 16, 128), F32),
    ((2, 8, 16, 128), F32),
)
SENDING = 6
EACH = 3
STRIDE = 45
VMEM_LIMIT = 60 * 1024 * 1024
SLABS = 16
COILS = 8
BATCH = 2


def kernel(image, cot, sens, labels, *rest):
    weights = rest[: len(WEIGHTS)]
    out = rest[len(WEIGHTS)]
    held = rest[len(WEIGHTS) + 1 : 2 * len(WEIGHTS) + 1]
    scratch = rest[2 * len(WEIGHTS) + 1 :]
    w = Refs(**dict(zip(WEIGHTS, held)), **dict(zip(WORK, scratch)))
    (col, lab, piece, sens_all, own_cot, cot_all, line_parts, halo, final) = (
        scratch[len(WORK) : len(WORK) + len(BUFFERS)]
    )
    sems, sens_sem, ready = scratch[len(WORK) + len(BUFFERS) :]
    (own_sem, field_sem, col_sem, cot_sem, line_sem, halo_sem, out_sem, send_sem, sens_send_sem) = [
        sems.at[i] for i in range(9)
    ]
    s = lax.axis_index("slab")
    c = lax.axis_index("coil")
    sends = []

    def send(source, target, recv, device):
        copy = pltpu.make_async_remote_copy(
            src_ref=source, dst_ref=target, send_sem=send_sem, recv_sem=recv,
            device_id=device, device_id_type=MESH,
        )
        copy.start()
        sends.append(copy)

    def local(source, target, sem):
        pltpu.make_async_copy(source, target, sem).start()

    def await_bytes(ref, sem):
        pltpu.make_async_copy(ref, ref, sem).wait()

    def span(start, size, step):
        return pl.ds(pl.multiple_of(start, step), size)

    barrier = pltpu.get_barrier_semaphore()
    for d in range(1, SLABS):
        pl.semaphore_signal(barrier, inc=1, device_id={"slab": lax.rem(s + d, SLABS)}, device_id_type=MESH)
    for d in range(1, COILS):
        pl.semaphore_signal(barrier, inc=1, device_id={"coil": lax.rem(c + d, COILS)}, device_id_type=MESH)
    halves = [span(lax.rem(16 * c + 8 + 8 * half, 128), 8, 8) for half in range(2)]
    places = [slice(8 * half, 8 * half + 8) for half in range(2)]
    for xs, place in zip(halves, places):
        local(cot.at[:, :, xs, :], own_cot.at[:, :, place, :], field_sem)
    for source, target in zip(weights, held):
        local(source, target, own_sem)
    local(labels.at[:, span(8 * c, 8, 8), :], lab, own_sem)
    for arr, field in enumerate((image, cot)):
        for xs, place in zip(halves, places):
            local(field.at[:, 4:8, xs, :], col.at[arr, :, 0:4, place, :], col_sem)
    pl.semaphore_wait(barrier, SLABS + COILS - 2)
    for d in range(1, SLABS):
        pl.semaphore_signal(ready, inc=1, device_id={"slab": lax.rem(s + d, SLABS)}, device_id_type=MESH)
    mine = pl.ds(pl.multiple_of(8 * s, 8), 8)
    for d in range(1, SLABS):
        t = lax.rem(s + d, SLABS)
        send(cot.at[:, :, lax.rem(16 * c + 8 + t, 128), :], cot_all.at[:, mine, :], cot_sem, {"slab": t})
    local(cot.at[:, :, lax.rem(16 * c + 8 + s, 128), :], cot_all.at[:, mine, :], cot_sem)
    below = lax.rem(s + SLABS - 1, SLABS)
    above = lax.rem(s + 1, SLABS)
    for arr, field in enumerate((image, cot)):
        for xs, place in zip(halves, places):
            send(field.at[:, 0:4, xs, :], col.at[arr, :, 4:8, place, :], col_sem, {"slab": below})

    def send_line(slab, coil):
        pltpu.make_async_remote_copy(
            src_ref=sens.at[:, :, :, lax.rem(16 * coil + 8 + slab, 128), :],
            dst_ref=sens_all.at[c, :, :, mine, :],
            send_sem=sens_send_sem,
            recv_sem=sens_sem.at[c],
            device_id={"slab": slab, "coil": coil},
            device_id_type=MESH,
        ).start()

    local(sens.at[:, :, :, lax.rem(16 * c + 8 + s, 128), :], sens_all.at[c, :, :, mine, :], sens_sem.at[c])
    lax.fori_loop(1, SLABS, lambda d, carry: (send_line(lax.rem(s + d, SLABS), c), carry)[1], 0)
    pl.semaphore_wait(ready, SLABS - 1)

    others = SLABS * (COILS - 1)
    share = EACH * HEADS * (TOKENS // CHUNK)

    def send_other(k):
        d = lax.rem(STRIDE * k + 7, others)
        send_line(lax.rem(s + lax.rem(d, SLABS), SLABS), lax.rem(c + 1 + d // SLABS, COILS))

    for k in range(others - share * SENDING):
        send_other(k)

    for target in held:
        await_bytes(target, own_sem)
    await_bytes(lab, own_sem)
    prepare_weights(w)
    w.kept[...] = jnp.transpose(w.mask[...].astype(F32))
    await_bytes(col, col_sem)
    prepare_fields(col, lab, w)

    def windows(first, last):
        lax.fori_loop(first, last, lambda win, carry: (one_window(win, w), carry)[1], 0)

    def window_and_sends(win, carry):
        first = others - share * SENDING + share * win

        def beside(step):
            for k in range(EACH):
                send_other(first + EACH * step + k)

        one_window(win, w, beside)
        return carry

    lax.fori_loop(0, SENDING, window_and_sends, 0)
    await_bytes(cot_all, cot_sem)
    w.line[...] = jnp.zeros((2, 128, 128), F32)
    for first in range(0, COILS, BATCH):
        for group in range(first, first + BATCH):
            await_bytes(sens_all.at[group], sens_sem.at[group])
        real, imag = some_coils(sens_all.at[first : first + BATCH], cot_all, w)
        w.line[0] += real
        w.line[1] += imag
    for d in range(1, SLABS):
        t = lax.rem(s + d, SLABS)
        send(w.line.at[:, span(8 * t, 8, 8), :], line_parts.at[s], line_sem, {"slab": t})
    local(w.line.at[:, mine, :], line_parts.at[s], line_sem)
    windows(SENDING, WINDOWS)
    finish_fields(piece, w)
    send(piece.at[:, 4:8], halo, halo_sem, {"slab": above})
    await_bytes(line_parts, line_sem)
    rows = final.reshape(256, 128)
    parts = line_parts.reshape(16, 16, 128)
    for x in range(16):
        rows[pl.ds(x, 16, stride=16), :] = parts[x] * -STEP_SIZE
    await_bytes(own_cot, field_sem)
    final[...] = final[...] + own_cot[...]
    final[:, 4:8] = final[:, 4:8] + piece[:, 0:4]
    await_bytes(halo, halo_sem)
    final[:, 0:4] = final[:, 0:4] + halo[...]
    for d in range(1, COILS):
        t = lax.rem(c + d, COILS)
        for xs, place in zip(halves, places):
            send(final.at[:, :, place, :], out.at[:, :, xs, :], out_sem, {"coil": t})
    for xs, place in zip(halves, places):
        local(final.at[:, :, place, :], out.at[:, :, xs, :], out_sem)
    await_bytes(sens_all.at[0:7], sens_send_sem)
    await_bytes(sens_all.at[7, :, :, 0:120, :], sens_send_sem)
    await_bytes(out, out_sem)
    for copy in sends:
        copy.wait_send()


def body(image, cotangent, sens, mask, labels, embed_weight, ln_gain, qkv_weight, proj_weight, unembed_weight):
    wide, narrow = selections()
    anywhere = pl.BlockSpec(memory_space=pl.ANY)
    scratch = [pltpu.VMEM(shape, dtype) for held in (WEIGHTS, WORK) for shape, dtype in held.values()]
    scratch += [pltpu.VMEM(shape, dtype) for shape, dtype in BUFFERS]
    scratch += [
        pltpu.SemaphoreType.DMA((9,)),
        pltpu.SemaphoreType.DMA((COILS,)),
        pltpu.SemaphoreType.REGULAR,
    ]
    return pl.pallas_call(
        kernel,
        out_shape=jax.ShapeDtypeStruct(image.shape, F32),
        in_specs=[anywhere] * (4 + len(WEIGHTS)),
        out_specs=anywhere,
        scratch_shapes=scratch,
        compiler_params=pltpu.CompilerParams(
            collective_id=0, has_side_effects=True, vmem_limit_bytes=VMEM_LIMIT
        ),
    )(
        image, cotangent, sens, labels, mask, embed_weight, ln_gain.reshape(1, CHANNELS), qkv_weight,
        proj_weight, unembed_weight.T, jnp.asarray(wide), jnp.asarray(narrow), jnp.asarray(dft_tables(128)),
    )


def solution(mesh):
    placed = (
        P(None, "slab", None, None),
        P(None, "slab", None, None),
        P("coil", None, "slab", None, None),
        P(),
        P("slab", None, None),
        P(),
        P(),
        P(),
        P(),
        P(),
    )
    return jax.shard_map(
        body, mesh=mesh, in_specs=placed, out_specs=P(None, "slab", None, None), check_vma=False
    )
```

```python
import functools

import jax
import jax.numpy as jnp
import numpy as np
from jax import lax
from jax.experimental import pallas as pl
from jax.experimental.pallas import tpu as pltpu
from jax.sharding import PartitionSpec as P

MESH = pl.DeviceIdType.MESH
F32 = jnp.float32
BF16 = jnp.bfloat16
HEADS = 3
HEAD = 32
CHANNELS = 96
WINDOWS = 8
TOKENS = 512
GROUPS = 4
CHUNK = 256
EPSILON = 1e-5
STEP_SIZE = 0.5
SCALE = HEAD ** -0.5
PENALTY = 1e9


def dft_tables(length):
    index = np.arange(length)
    angle = (index[:, None] * index[None, :] % length) * (2.0 * np.pi / length)
    cos = np.cos(angle) / np.sqrt(length)
    sin = np.sin(angle) / np.sqrt(length)
    forward = np.block([[cos, sin], [-sin, cos]])
    high = forward.astype(jnp.bfloat16)
    low = (forward - high.astype(np.float64)).astype(jnp.bfloat16)
    return np.stack([high, low, np.ascontiguousarray(high.T), np.ascontiguousarray(low.T)])


def selections():
    select = np.zeros((GROUPS, 8, 32), np.float32)
    for t in range(GROUPS):
        for f in range(8):
            part, px, py = f // 4, f // 2 % 2, f % 2
            select[t, f, part * 16 + px * 8 + 2 * t + py] = 1.0
    wide = np.zeros((3, GROUPS, 8, 192), np.float32)
    for slot, piece in enumerate((0, 0, 0, 1, 1, 2)):
        wide[piece, :, :, 32 * slot : 32 * slot + 32] = select
    return wide, np.ascontiguousarray(select.transpose(0, 2, 1))


def dot(left, right):
    return jnp.dot(left, right, preferred_element_type=F32)


def split2(value):
    high = value.astype(BF16)
    return high, (value - high.astype(F32)).astype(BF16)


def split3(value):
    high = value.astype(BF16)
    rest = value - high.astype(F32)
    middle = rest.astype(BF16)
    return high, middle, (rest - middle.astype(F32)).astype(BF16)


def lane_index(shape):
    return lax.broadcasted_iota(jnp.int32, shape, len(shape) - 1)


def prepare_weights(w):
    wide, narrow = w.wide, w.narrow
    emb = w.embed[...]
    w.pad[...] = jnp.zeros((128, 384), F32)
    w.pad[0:8, 0:CHANNELS] = emb
    w.pad[8:16, 0:CHANNELS] = jnp.broadcast_to(w.gain[...], (8, CHANNELS))
    w.pad[16:24, 0:CHANNELS] = w.unembed[...]
    turned = jnp.transpose(w.pad[:, 0:128])
    w.gain_col[...] = jnp.broadcast_to(turned[0:CHANNELS, 8:9], (CHANNELS, 128))
    emb_t = split3(turned[0:CHANNELS, 0:8])
    un = split3(turned[0:CHANNELS, 16:24])
    emb_pieces = split2(emb)
    for t in range(GROUPS):
        w.to_embed[t] = sum(dot(p.astype(F32), wide[i, t]) for i, p in enumerate(emb_t)).astype(BF16)
        w.to_mixed[t] = sum(dot(p.astype(F32), wide[i, t]) for i, p in enumerate(un)).astype(BF16)
        for i, p in enumerate(emb_pieces):
            w.from_embed[i, t] = dot(narrow[t], p.astype(F32)).astype(BF16)
    w.pad[0:CHANNELS, 0:288] = w.qkv[...].astype(F32)
    for b in range(3):
        w.qkv_t[128 * b : 128 * b + 128, :] = jnp.transpose(w.pad[:, 128 * b : 128 * b + 128]).astype(BF16)


def prepare_fields(col, lab, w):
    rows = col.reshape(2, 2, 128, 128)
    low = lane_index((8, 128)) < 64
    for part in range(2):
        for px in range(2):
            both = jnp.concatenate(
                [rows[arr, part, pl.ds(px, 64, stride=2), :] for arr in range(2)], 0
            )
            w.turn[...] = jnp.transpose(both)
            place = 8 * (part * 2 + px)
            for win in range(WINDOWS):
                first = w.turn[8 * ((2 * win + 1) % 16) : 8 * ((2 * win + 1) % 16) + 8, :]
                second = w.turn[8 * ((2 * win + 2) % 16) : 8 * ((2 * win + 2) % 16) + 8, :]
                w.field[win, 0, place : place + 8, :] = jnp.where(low, first, pltpu.roll(second, 64, 1))
                w.field[win, 1, place : place + 8, :] = jnp.where(low, pltpu.roll(first, 64, 1), second)
    w.pad[:, 0:128] = jnp.zeros((128, 128), F32)
    for z in range(8):
        w.pad[8 * z : 8 * z + 8, 0:64] = lab[z].astype(F32)
    w.turn[...] = jnp.transpose(w.pad[:, 0:128])
    for win in range(WINDOWS):
        tile = w.turn[8 * win : 8 * win + 8, :]
        moved = pltpu.roll(pltpu.roll(tile, 4, 0), 64, 1)
        w.label[win] = jnp.where(low, tile, moved)


def one_window(win, w, beside=None):
    image6 = split3(w.field[win, 0])
    grad6 = split3(w.field[win, 1])
    order = (0, 1, 2, 0, 1, 0)
    image6 = jnp.concatenate([image6[i] for i in order], 0)
    grad6 = jnp.concatenate([grad6[i] for i in order], 0)
    embedded = jnp.concatenate([dot(w.to_embed[t], image6) for t in range(GROUPS)], 1)
    mixed = jnp.concatenate([dot(w.to_mixed[t], grad6) for t in range(GROUPS)], 1)
    label = w.label[win]
    label = jnp.concatenate([label[t : t + 1, :] for t in range(GROUPS)], 1)

    gain = jnp.concatenate([w.gain_col[...]] * GROUPS, 1)
    mean = jnp.sum(embedded, 0, keepdims=True) * (1.0 / CHANNELS)
    centered = embedded - mean
    variance = jnp.sum(centered * centered, 0, keepdims=True) * (1.0 / CHANNELS)
    inverse = lax.rsqrt(variance + EPSILON)
    unit = centered * inverse
    w.unit[...] = unit
    normed = (unit * gain).astype(BF16)
    projected = dot(w.qkv_t[0:288, :][:, 0:CHANNELS], normed).astype(BF16).astype(F32)
    proj = w.proj[...]
    mixed_high, mixed_low = split2(mixed)
    attended = (dot(proj, mixed_high) + dot(proj, mixed_low)).astype(BF16).astype(F32)
    w.mixed[...] = mixed

    row = lax.broadcasted_iota(jnp.int32, (HEAD, TOKENS), 0)
    zero_f = jnp.zeros((HEAD, TOKENS), F32)
    zero = zero_f.astype(BF16)
    label_key = jnp.where(row == 0, label, jnp.where(row == 1, 1.0 - label, 0.0))
    label_query = jnp.where(row == 0, label - 1.0, jnp.where(row == 1, -label, 0.0)) * PENALTY
    label_query = label_query.astype(BF16)
    lane = lane_index((1, 128))
    only_query = ((lane >= 64) & (lane < 96)).astype(F32)
    only_grad = (lane >= 96).astype(F32)
    lane_scale = jnp.where(lane < 96, SCALE, 1.0).astype(F32)

    def head_operands(head):
        at = HEAD * head
        query = projected[at : at + HEAD]
        key = projected[CHANNELS + at : CHANNELS + at + HEAD]
        value = projected[2 * CHANNELS + at : 2 * CHANNELS + at + HEAD]
        grad = attended[at : at + HEAD]
        token = jnp.transpose(jnp.concatenate([key, value, query, grad], 0))
        more = jnp.transpose(jnp.concatenate([key, key, label_key, zero_f], 0))
        token_query = (token * only_query).astype(BF16)
        token_grad = (token * only_grad).astype(BF16)
        token = token.astype(BF16)
        left = jnp.concatenate([token, more.astype(BF16)], 1)
        parts = split3(query * (SCALE * float(np.log2(np.e))))
        right = jnp.concatenate(
            [parts[0], zero, zero, zero, parts[1], parts[2], label_query, zero], 0
        )
        right_value = jnp.concatenate([zero, grad.astype(BF16), zero, zero], 0)
        return left, right, token, right_value, key.astype(BF16), token_grad, token_query

    def products(operands, chunk):
        left, right, token, right_value = operands[:4]
        cut = slice(CHUNK * chunk, CHUNK * chunk + CHUNK)
        scores = dot(left, right[:, cut])
        return scores, dot(token, right_value[:, cut]).astype(BF16)

    chunks = TOKENS // CHUNK
    steps = [(head, chunk) for head in range(HEADS) for chunk in range(chunks)]
    operands = {0: head_operands(0)}
    ahead = [products(operands[0], 0)]
    for index, (head, chunk) in enumerate(steps):
        at = HEAD * head
        cut = slice(CHUNK * chunk, CHUNK * chunk + CHUNK)
        scores, d_soft = ahead.pop(0)
        if beside is not None:
            beside(index)
        if index + 1 < len(steps):
            after, after_chunk = steps[index + 1]
            if after not in operands:
                operands[after] = head_operands(after)
            ahead.append(products(operands[after], after_chunk))
        key16, token_grad, token_query = operands[head][4:]
        top = jnp.max(scores, 0, keepdims=True)
        weights = jnp.exp2(scores - top)
        soft = weights * (1.0 / jnp.sum(weights, 0, keepdims=True))
        d_soft = d_soft.astype(F32)
        inner = jnp.sum(d_soft * soft, 0, keepdims=True)
        d_scores = (soft * (d_soft - inner)).astype(BF16)
        w.d_proj[at : at + HEAD, cut] = dot(key16, d_scores) * SCALE
        part = dot(soft.astype(BF16), token_grad[cut, :]) + dot(d_scores, token_query[cut, :])
        total = part if chunk == 0 else total + part
        if chunk == chunks - 1:
            turned = jnp.transpose(total * lane_scale)
            w.d_proj[CHANNELS + at : CHANNELS + at + HEAD, :] = turned[64:96]
            w.d_proj[2 * CHANNELS + at : 2 * CHANNELS + at + HEAD, :] = turned[96:128]

    d_normed = dot(w.qkv[...], w.d_proj[...].astype(BF16)).astype(BF16).astype(F32)
    d_unit = d_normed * gain
    unit = w.unit[...]
    first = jnp.sum(d_unit, 0, keepdims=True) * (1.0 / CHANNELS)
    second = jnp.sum(d_unit * unit, 0, keepdims=True) * (1.0 / CHANNELS)
    d_embedded = inverse * (d_unit - first - unit * second) + w.mixed[...]
    high, low = split2(d_embedded)
    result = jnp.zeros((32, 128), F32)
    for t in range(GROUPS):
        cut = slice(128 * t, 128 * t + 128)
        result += dot(w.from_embed[0, t], high[:, cut])
        result += dot(w.from_embed[0, t], low[:, cut])
        result += dot(w.from_embed[1, t], high[:, cut])
    w.d_field[win] = result


def finish_fields(piece, w):
    rows = piece.reshape(2, 128, 128)
    low = lane_index((8, 128)) < 64
    for px in range(2):
        for win in range(WINDOWS):
            real = w.d_field[win, 8 * px : 8 * px + 8, :]
            imag = w.d_field[win, 16 + 8 * px : 24 + 8 * px, :]
            first = 8 * ((2 * win + 1) % 16)
            second = 8 * ((2 * win + 2) % 16)
            w.turn[first : first + 8, :] = jnp.where(low, real, pltpu.roll(imag, 64, 1))
            w.turn[second : second + 8, :] = jnp.where(low, pltpu.roll(real, 64, 1), imag)
        turned = jnp.transpose(w.turn[...])
        for part in range(2):
            rows[part, pl.ds(px, 64, stride=2), :] = turned[64 * part : 64 * part + 64, :]


def product3(left, right):
    return dot(left[0], right[0]) + dot(left[1], right[0]) + dot(left[0], right[1])


def turned(value, count):
    blocks = []
    for coil in range(count):
        rows = slice(128 * coil, 128 * coil + 128)
        blocks.append(
            jnp.concatenate([jnp.transpose(value[rows, 0:128]), jnp.transpose(value[rows, 128:256])], 1)
        )
    return jnp.concatenate(blocks, 0)


def some_coils(sens, cot, w):
    coils = [sens[group, k] for group in range(sens.shape[0]) for k in range(2)]
    count = len(coils)
    g_real, g_imag = cot[0], cot[1]
    real = jnp.concatenate([s[0] * g_real - s[1] * g_imag for s in coils], 0)
    imag = jnp.concatenate([s[0] * g_imag + s[1] * g_real for s in coils], 0)
    forward = (w.tables[2], w.tables[3])
    backward = (w.tables[0], w.tables[1])
    value = turned(product3(split2(jnp.concatenate([real, imag], 1)), forward), count)
    value = product3(split2(value), forward)
    kept = jnp.concatenate([w.kept[...]] * count, 0)
    value = value * jnp.concatenate([kept, kept], 1)
    value = turned(product3(split2(value), backward), count)
    value = product3(split2(value), backward)
    real = sum(
        s[0] * value[128 * k : 128 * k + 128, 0:128] + s[1] * value[128 * k : 128 * k + 128, 128:256]
        for k, s in enumerate(coils)
    )
    imag = sum(
        s[0] * value[128 * k : 128 * k + 128, 128:256] - s[1] * value[128 * k : 128 * k + 128, 0:128]
        for k, s in enumerate(coils)
    )
    return real, imag


class Refs:
    def __init__(self, **refs):
        self.__dict__.update(refs)


WEIGHTS = dict(
    mask=((128, 128), jnp.int32),
    embed=((8, CHANNELS), F32),
    gain=((1, CHANNELS), F32),
    qkv=((CHANNELS, 288), BF16),
    proj=((CHANNELS, CHANNELS), BF16),
    unembed=((8, CHANNELS), F32),
    wide=((3, GROUPS, 8, 192), F32),
    narrow=((GROUPS, 32, 8), F32),
    tables=((4, 256, 256), BF16),
)
WORK = dict(
    pad=((128, 384), F32),
    gain_col=((CHANNELS, 128), F32),
    to_embed=((GROUPS, CHANNELS, 192), BF16),
    to_mixed=((GROUPS, CHANNELS, 192), BF16),
    from_embed=((2, GROUPS, 32, CHANNELS), BF16),
    qkv_t=((384, 128), BF16),
    turn=((128, 128), F32),
    field=((WINDOWS, 2, 32, 128), F32),
    label=((WINDOWS, 8, 128), F32),
    unit=((CHANNELS, TOKENS), F32),
    mixed=((CHANNELS, TOKENS), F32),
    d_proj=((288, TOKENS), F32),
    d_field=((WINDOWS, 32, 128), F32),
    kept=((128, 128), F32),
    line=((2, 128, 128), F32),
)
BUFFERS = (
    ((2, 2, 8, 16, 128), F32),
    ((8, 8, 64), jnp.int32),
    ((2, 8, 16, 128), F32),
    ((8, 2, 2, 128, 128), F32),
    ((2, 8, 16, 128), F32),
    ((2, 128, 128), F32),
    ((16, 2, 8, 128), F32),
    ((2, 4, 16, 128), F32),
    ((2, 8, 16, 128), F32),
    ((2, 8, 128, 128), F32),
)
SENDING = 7
EACH = 3
STRIDE = 45
VMEM_LIMIT = 60 * 1024 * 1024
SLABS = 16
COILS = 8
BATCH = 4
RING = 4


def kernel(image, cot, sens, labels, *rest):
    weights = rest[: len(WEIGHTS)]
    out = rest[len(WEIGHTS)]
    held = rest[len(WEIGHTS) + 1 : 2 * len(WEIGHTS) + 1]
    scratch = rest[2 * len(WEIGHTS) + 1 :]
    w = Refs(**dict(zip(WEIGHTS, held)), **dict(zip(WORK, scratch)))
    (col, lab, piece, sens_all, own_cot, cot_all, line_parts, halo, final, gathered) = (
        scratch[len(WORK) : len(WORK) + len(BUFFERS)]
    )
    sems, sens_sem, ag_sems, ready = scratch[len(WORK) + len(BUFFERS) :]
    (own_sem, field_sem, col_sem, cot_sem, line_sem, halo_sem, out_sem, send_sem, sens_send_sem) = [
        sems.at[i] for i in range(9)
    ]
    y_sem, right_sem, left_sem, far_sem, right2_sem, left2_sem, far2_sem = [ag_sems.at[i] for i in range(7)]
    s = lax.axis_index("slab")
    c = lax.axis_index("coil")
    sends = []

    def send(source, target, recv, device):
        copy = pltpu.make_async_remote_copy(
            src_ref=source, dst_ref=target, send_sem=send_sem, recv_sem=recv,
            device_id=device, device_id_type=MESH,
        )
        copy.start()
        sends.append(copy)

    def local(source, target, sem):
        pltpu.make_async_copy(source, target, sem).start()

    def await_bytes(ref, sem):
        pltpu.make_async_copy(ref, ref, sem).wait()

    def span(start, size, step):
        return pl.ds(pl.multiple_of(start, step), size)

    barrier = pltpu.get_barrier_semaphore()
    for d in range(1, SLABS):
        pl.semaphore_signal(barrier, inc=1, device_id={"slab": lax.rem(s + d, SLABS)}, device_id_type=MESH)
    for d in range(1, COILS):
        pl.semaphore_signal(barrier, inc=1, device_id={"coil": lax.rem(c + d, COILS)}, device_id_type=MESH)
    halves = [span(lax.rem(16 * c + 8 + 8 * half, 128), 8, 8) for half in range(2)]
    places = [slice(8 * half, 8 * half + 8) for half in range(2)]
    for xs, place in zip(halves, places):
        local(cot.at[:, :, xs, :], own_cot.at[:, :, place, :], field_sem)
    for source, target in zip(weights, held):
        local(source, target, own_sem)
    local(labels.at[:, span(8 * c, 8, 8), :], lab, own_sem)
    for arr, field in enumerate((image, cot)):
        for xs, place in zip(halves, places):
            local(field.at[:, 4:8, xs, :], col.at[arr, :, 0:4, place, :], col_sem)
    pl.semaphore_wait(barrier, SLABS + COILS - 2)
    for d in range(1, SLABS):
        pl.semaphore_signal(ready, inc=1, device_id={"slab": lax.rem(s + d, SLABS)}, device_id_type=MESH)
    mine = pl.ds(pl.multiple_of(8 * s, 8), 8)
    for d in range(1, SLABS):
        t = lax.rem(s + d, SLABS)
        send(cot.at[:, :, lax.rem(16 * c + 8 + t, 128), :], cot_all.at[:, mine, :], cot_sem, {"slab": t})
    local(cot.at[:, :, lax.rem(16 * c + 8 + s, 128), :], cot_all.at[:, mine, :], cot_sem)
    below = lax.rem(s + SLABS - 1, SLABS)
    above = lax.rem(s + 1, SLABS)
    for arr, field in enumerate((image, cot)):
        for xs, place in zip(halves, places):
            send(field.at[:, 0:4, xs, :], col.at[arr, :, 4:8, place, :], col_sem, {"slab": below})

    def send_line(slab, coil):
        pltpu.make_async_remote_copy(
            src_ref=sens.at[:, :, :, lax.rem(16 * coil + 8 + slab, 128), :],
            dst_ref=sens_all.at[c, :, :, mine, :],
            send_sem=sens_send_sem,
            recv_sem=sens_sem.at[c],
            device_id={"slab": slab, "coil": coil},
            device_id_type=MESH,
        ).start()

    local(sens.at[:, :, :, lax.rem(16 * c + 8 + s, 128), :], sens_all.at[c, :, :, mine, :], sens_sem.at[c])
    pl.semaphore_wait(ready, SLABS - 1)

    others = SLABS * COILS - 1
    share = EACH * HEADS * (TOKENS // CHUNK)

    def send_other(k):
        d = lax.rem(STRIDE * k + 7, others) + 1
        send_line(lax.rem(s + lax.rem(d, SLABS), SLABS), lax.rem(c + d // SLABS, COILS))

    for k in range(others - share * SENDING):
        send_other(k)

    for target in held:
        await_bytes(target, own_sem)
    await_bytes(lab, own_sem)
    prepare_weights(w)
    w.kept[...] = jnp.transpose(w.mask[...].astype(F32))
    await_bytes(col, col_sem)
    prepare_fields(col, lab, w)

    def windows(first, last):
        lax.fori_loop(first, last, lambda win, carry: (one_window(win, w), carry)[1], 0)

    def window_and_sends(win, carry):
        first = others - share * SENDING + share * win

        def beside(step):
            for k in range(EACH):
                send_other(first + EACH * step + k)

        one_window(win, w, beside)
        return carry

    lax.fori_loop(0, SENDING, window_and_sends, 0)
    await_bytes(cot_all, cot_sem)
    w.line[...] = jnp.zeros((2, 128, 128), F32)
    for first in range(0, COILS, BATCH):
        for group in range(first, first + BATCH):
            await_bytes(sens_all.at[group], sens_sem.at[group])
        real, imag = some_coils(sens_all.at[first : first + BATCH], cot_all, w)
        w.line[0] += real
        w.line[1] += imag
    for d in range(1, SLABS):
        t = lax.rem(s + d, SLABS)
        send(w.line.at[:, span(8 * t, 8, 8), :], line_parts.at[s], line_sem, {"slab": t})
    local(w.line.at[:, mine, :], line_parts.at[s], line_sem)
    windows(SENDING, WINDOWS)
    finish_fields(piece, w)
    send(piece.at[:, 4:8], halo, halo_sem, {"slab": above})
    await_bytes(line_parts, line_sem)
    rows = final.reshape(256, 128)
    parts = line_parts.reshape(16, 16, 128)
    for x in range(16):
        rows[pl.ds(x, 16, stride=16), :] = parts[x] * -STEP_SIZE
    await_bytes(own_cot, field_sem)
    final[...] = final[...] + own_cot[...]
    final[:, 4:8] = final[:, 4:8] + piece[:, 0:4]
    await_bytes(halo, halo_sem)
    final[:, 0:4] = final[:, 0:4] + halo[...]
    high = c // RING
    across = lax.rem(c, RING)
    right = RING * high + lax.rem(across + 1, RING)
    left = RING * high + lax.rem(across + RING - 1, RING)
    other = lax.rem(c + RING, COILS)

    def column(coil, half):
        return gathered.at[:, :, span(lax.rem(16 * coil + 8 + 8 * half, 128), 8, 8), :]

    def pass_on(coil, half, target, sem):
        block = column(coil, half)
        send(block, block, sem, {"coil": target})

    for half in range(2):
        gathered[:, :, halves[half], :] = final[:, :, places[half], :]
    for half in range(2):
        pass_on(c, half, other, y_sem)
    for half in (0, 1):
        pass_on(c, half, right, right_sem)
        pass_on(c, 1 - half, left, left_sem)
    two = final.at[:, :, 0:16, :]
    one = final.at[:, :, 0:8, :]
    await_bytes(two, y_sem)
    await_bytes(two, right_sem)
    await_bytes(two, left_sem)
    pass_on(left, 0, right, far_sem)
    pass_on(right, 1, left, far_sem)
    across_right = lax.rem(right + RING, COILS)
    across_left = lax.rem(left + RING, COILS)
    for half in (0, 1):
        pass_on(other, half, right, right2_sem)
        pass_on(other, 1 - half, left, left2_sem)
    await_bytes(two, right2_sem)
    await_bytes(two, left2_sem)
    pass_on(across_left, 0, right, far2_sem)
    pass_on(across_right, 1, left, far2_sem)
    await_bytes(two, far_sem)
    await_bytes(two, far2_sem)
    local(gathered, out, out_sem)
    await_bytes(sens_all.at[0:7], sens_send_sem)
    await_bytes(sens_all.at[7, :, :, 0:120, :], sens_send_sem)
    await_bytes(out, out_sem)
    for copy in sends:
        copy.wait_send()


def body(image, cotangent, sens, mask, labels, embed_weight, ln_gain, qkv_weight, proj_weight, unembed_weight):
    wide, narrow = selections()
    anywhere = pl.BlockSpec(memory_space=pl.ANY)
    scratch = [pltpu.VMEM(shape, dtype) for held in (WEIGHTS, WORK) for shape, dtype in held.values()]
    scratch += [pltpu.VMEM(shape, dtype) for shape, dtype in BUFFERS]
    scratch += [
        pltpu.SemaphoreType.DMA((9,)),
        pltpu.SemaphoreType.DMA((COILS,)),
        pltpu.SemaphoreType.DMA((7,)),
        pltpu.SemaphoreType.REGULAR,
    ]
    return pl.pallas_call(
        kernel,
        out_shape=jax.ShapeDtypeStruct(image.shape, F32),
        in_specs=[anywhere] * (4 + len(WEIGHTS)),
        out_specs=anywhere,
        scratch_shapes=scratch,
        compiler_params=pltpu.CompilerParams(
            collective_id=0, has_side_effects=True, vmem_limit_bytes=VMEM_LIMIT
        ),
    )(
        image, cotangent, sens, labels, mask, embed_weight, ln_gain.reshape(1, CHANNELS), qkv_weight,
        proj_weight, unembed_weight.T, jnp.asarray(wide), jnp.asarray(narrow), jnp.asarray(dft_tables(128)),
    )


def solution(mesh):
    placed = (
        P(None, "slab", None, None),
        P(None, "slab", None, None),
        P("coil", None, "slab", None, None),
        P(),
        P("slab", None, None),
        P(),
        P(),
        P(),
        P(),
        P(),
    )
    return jax.shard_map(
        body, mesh=mesh, in_specs=placed, out_specs=P(None, "slab", None, None), check_vma=False
    )
```

```python
import functools

import jax
import jax.numpy as jnp
import numpy as np
from jax import lax
from jax.experimental import pallas as pl
from jax.experimental.pallas import tpu as pltpu
from jax.sharding import PartitionSpec as P

MESH = pl.DeviceIdType.MESH
F32 = jnp.float32
BF16 = jnp.bfloat16
HEADS = 3
HEAD = 32
CHANNELS = 96
WINDOWS = 8
TOKENS = 512
GROUPS = 4
CHUNK = 256
EPSILON = 1e-5
STEP_SIZE = 0.5
SCALE = HEAD ** -0.5
PENALTY = 1e9


def dft_tables(length):
    index = np.arange(length)
    angle = (index[:, None] * index[None, :] % length) * (2.0 * np.pi / length)
    cos = np.cos(angle) / np.sqrt(length)
    sin = np.sin(angle) / np.sqrt(length)
    forward = np.block([[cos, sin], [-sin, cos]])
    high = forward.astype(jnp.bfloat16)
    low = (forward - high.astype(np.float64)).astype(jnp.bfloat16)
    return np.stack([high, low, np.ascontiguousarray(high.T), np.ascontiguousarray(low.T)])


def selections():
    select = np.zeros((GROUPS, 8, 32), np.float32)
    for t in range(GROUPS):
        for f in range(8):
            part, px, py = f // 4, f // 2 % 2, f % 2
            select[t, f, part * 16 + px * 8 + 2 * t + py] = 1.0
    wide = np.zeros((3, GROUPS, 8, 192), np.float32)
    for slot, piece in enumerate((0, 0, 0, 1, 1, 2)):
        wide[piece, :, :, 32 * slot : 32 * slot + 32] = select
    return wide, np.ascontiguousarray(select.transpose(0, 2, 1))


def dot(left, right):
    return jnp.dot(left, right, preferred_element_type=F32)


def split2(value):
    high = value.astype(BF16)
    return high, (value - high.astype(F32)).astype(BF16)


def split3(value):
    high = value.astype(BF16)
    rest = value - high.astype(F32)
    middle = rest.astype(BF16)
    return high, middle, (rest - middle.astype(F32)).astype(BF16)


def lane_index(shape):
    return lax.broadcasted_iota(jnp.int32, shape, len(shape) - 1)


def prepare_weights(w):
    wide, narrow = w.wide, w.narrow
    emb = w.embed[...]
    w.pad[...] = jnp.zeros((128, 384), F32)
    w.pad[0:8, 0:CHANNELS] = emb
    w.pad[8:16, 0:CHANNELS] = jnp.broadcast_to(w.gain[...], (8, CHANNELS))
    w.pad[16:24, 0:CHANNELS] = w.unembed[...]
    turned = jnp.transpose(w.pad[:, 0:128])
    w.gain_col[...] = jnp.broadcast_to(turned[0:CHANNELS, 8:9], (CHANNELS, 128))
    emb_t = split3(turned[0:CHANNELS, 0:8])
    un = split3(turned[0:CHANNELS, 16:24])
    emb_pieces = split2(emb)
    for t in range(GROUPS):
        w.to_embed[t] = sum(dot(p.astype(F32), wide[i, t]) for i, p in enumerate(emb_t)).astype(BF16)
        w.to_mixed[t] = sum(dot(p.astype(F32), wide[i, t]) for i, p in enumerate(un)).astype(BF16)
        for i, p in enumerate(emb_pieces):
            w.from_embed[i, t] = dot(narrow[t], p.astype(F32)).astype(BF16)
    w.pad[0:CHANNELS, 0:288] = w.qkv[...].astype(F32)
    for b in range(3):
        w.qkv_t[128 * b : 128 * b + 128, :] = jnp.transpose(w.pad[:, 128 * b : 128 * b + 128]).astype(BF16)


def prepare_fields(col, lab, w):
    rows = col.reshape(2, 2, 128, 128)
    low = lane_index((8, 128)) < 64
    for part in range(2):
        for px in range(2):
            both = jnp.concatenate(
                [rows[arr, part, pl.ds(px, 64, stride=2), :] for arr in range(2)], 0
            )
            w.turn[...] = jnp.transpose(both)
            place = 8 * (part * 2 + px)
            for win in range(WINDOWS):
                first = w.turn[8 * ((2 * win + 1) % 16) : 8 * ((2 * win + 1) % 16) + 8, :]
                second = w.turn[8 * ((2 * win + 2) % 16) : 8 * ((2 * win + 2) % 16) + 8, :]
                w.field[win, 0, place : place + 8, :] = jnp.where(low, first, pltpu.roll(second, 64, 1))
                w.field[win, 1, place : place + 8, :] = jnp.where(low, pltpu.roll(first, 64, 1), second)
    w.pad[:, 0:128] = jnp.zeros((128, 128), F32)
    for z in range(8):
        w.pad[8 * z : 8 * z + 8, 0:64] = lab[z].astype(F32)
    w.turn[...] = jnp.transpose(w.pad[:, 0:128])
    for win in range(WINDOWS):
        tile = w.turn[8 * win : 8 * win + 8, :]
        moved = pltpu.roll(pltpu.roll(tile, 4, 0), 64, 1)
        w.label[win] = jnp.where(low, tile, moved)


def one_window(win, w, beside=None):
    image6 = split3(w.field[win, 0])
    grad6 = split3(w.field[win, 1])
    order = (0, 1, 2, 0, 1, 0)
    image6 = jnp.concatenate([image6[i] for i in order], 0)
    grad6 = jnp.concatenate([grad6[i] for i in order], 0)
    embedded = jnp.concatenate([dot(w.to_embed[t], image6) for t in range(GROUPS)], 1)
    mixed = jnp.concatenate([dot(w.to_mixed[t], grad6) for t in range(GROUPS)], 1)
    label = w.label[win]
    label = jnp.concatenate([label[t : t + 1, :] for t in range(GROUPS)], 1)

    gain = jnp.concatenate([w.gain_col[...]] * GROUPS, 1)
    mean = jnp.sum(embedded, 0, keepdims=True) * (1.0 / CHANNELS)
    centered = embedded - mean
    variance = jnp.sum(centered * centered, 0, keepdims=True) * (1.0 / CHANNELS)
    inverse = lax.rsqrt(variance + EPSILON)
    unit = centered * inverse
    w.unit[...] = unit
    normed = (unit * gain).astype(BF16)
    projected = dot(w.qkv_t[0:288, :][:, 0:CHANNELS], normed).astype(BF16).astype(F32)
    proj = w.proj[...]
    mixed_high, mixed_low = split2(mixed)
    attended = (dot(proj, mixed_high) + dot(proj, mixed_low)).astype(BF16).astype(F32)
    w.mixed[...] = mixed

    row = lax.broadcasted_iota(jnp.int32, (HEAD, TOKENS), 0)
    zero_f = jnp.zeros((HEAD, TOKENS), F32)
    zero = zero_f.astype(BF16)
    label_key = jnp.where(row == 0, label, jnp.where(row == 1, 1.0 - label, 0.0))
    label_query = jnp.where(row == 0, label - 1.0, jnp.where(row == 1, -label, 0.0)) * PENALTY
    label_query = label_query.astype(BF16)
    lane = lane_index((1, 128))
    only_query = ((lane >= 64) & (lane < 96)).astype(F32)
    only_grad = (lane >= 96).astype(F32)
    lane_scale = jnp.where(lane < 96, SCALE, 1.0).astype(F32)

    def head_operands(head):
        at = HEAD * head
        query = projected[at : at + HEAD]
        key = projected[CHANNELS + at : CHANNELS + at + HEAD]
        value = projected[2 * CHANNELS + at : 2 * CHANNELS + at + HEAD]
        grad = attended[at : at + HEAD]
        token = jnp.transpose(jnp.concatenate([key, value, query, grad], 0))
        more = jnp.transpose(jnp.concatenate([key, key, label_key, zero_f], 0))
        token_query = (token * only_query).astype(BF16)
        token_grad = (token * only_grad).astype(BF16)
        token = token.astype(BF16)
        left = jnp.concatenate([token, more.astype(BF16)], 1)
        parts = split3(query * (SCALE * float(np.log2(np.e))))
        right = jnp.concatenate(
            [parts[0], zero, zero, zero, parts[1], parts[2], label_query, zero], 0
        )
        right_value = jnp.concatenate([zero, grad.astype(BF16), zero, zero], 0)
        return left, right, token, right_value, key.astype(BF16), token_grad, token_query

    def products(operands, chunk):
        left, right, token, right_value = operands[:4]
        cut = slice(CHUNK * chunk, CHUNK * chunk + CHUNK)
        scores = dot(left, right[:, cut])
        return scores, dot(token, right_value[:, cut]).astype(BF16)

    chunks = TOKENS // CHUNK
    steps = [(head, chunk) for head in range(HEADS) for chunk in range(chunks)]
    operands = {0: head_operands(0)}
    ahead = [products(operands[0], 0)]
    for index, (head, chunk) in enumerate(steps):
        at = HEAD * head
        cut = slice(CHUNK * chunk, CHUNK * chunk + CHUNK)
        scores, d_soft = ahead.pop(0)
        if beside is not None:
            beside(index)
        if index + 1 < len(steps):
            after, after_chunk = steps[index + 1]
            if after not in operands:
                operands[after] = head_operands(after)
            ahead.append(products(operands[after], after_chunk))
        key16, token_grad, token_query = operands[head][4:]
        top = jnp.max(scores, 0, keepdims=True)
        weights = jnp.exp2(scores - top)
        soft = weights * (1.0 / jnp.sum(weights, 0, keepdims=True))
        d_soft = d_soft.astype(F32)
        inner = jnp.sum(d_soft * soft, 0, keepdims=True)
        d_scores = (soft * (d_soft - inner)).astype(BF16)
        w.d_proj[at : at + HEAD, cut] = dot(key16, d_scores) * SCALE
        part = dot(soft.astype(BF16), token_grad[cut, :]) + dot(d_scores, token_query[cut, :])
        total = part if chunk == 0 else total + part
        if chunk == chunks - 1:
            turned = jnp.transpose(total * lane_scale)
            w.d_proj[CHANNELS + at : CHANNELS + at + HEAD, :] = turned[64:96]
            w.d_proj[2 * CHANNELS + at : 2 * CHANNELS + at + HEAD, :] = turned[96:128]

    d_normed = dot(w.qkv[...], w.d_proj[...].astype(BF16)).astype(BF16).astype(F32)
    d_unit = d_normed * gain
    unit = w.unit[...]
    first = jnp.sum(d_unit, 0, keepdims=True) * (1.0 / CHANNELS)
    second = jnp.sum(d_unit * unit, 0, keepdims=True) * (1.0 / CHANNELS)
    d_embedded = inverse * (d_unit - first - unit * second) + w.mixed[...]
    high, low = split2(d_embedded)
    result = jnp.zeros((32, 128), F32)
    for t in range(GROUPS):
        cut = slice(128 * t, 128 * t + 128)
        result += dot(w.from_embed[0, t], high[:, cut])
        result += dot(w.from_embed[0, t], low[:, cut])
        result += dot(w.from_embed[1, t], high[:, cut])
    w.d_field[win] = result


def finish_fields(piece, w):
    rows = piece.reshape(2, 128, 128)
    low = lane_index((8, 128)) < 64
    for px in range(2):
        for win in range(WINDOWS):
            real = w.d_field[win, 8 * px : 8 * px + 8, :]
            imag = w.d_field[win, 16 + 8 * px : 24 + 8 * px, :]
            first = 8 * ((2 * win + 1) % 16)
            second = 8 * ((2 * win + 2) % 16)
            w.turn[first : first + 8, :] = jnp.where(low, real, pltpu.roll(imag, 64, 1))
            w.turn[second : second + 8, :] = jnp.where(low, pltpu.roll(real, 64, 1), imag)
        turned = jnp.transpose(w.turn[...])
        for part in range(2):
            rows[part, pl.ds(px, 64, stride=2), :] = turned[64 * part : 64 * part + 64, :]


def product3(left, right):
    return dot(left[0], right[0]) + dot(left[1], right[0]) + dot(left[0], right[1])


def turned(value, count):
    blocks = []
    for coil in range(count):
        rows = slice(128 * coil, 128 * coil + 128)
        blocks.append(
            jnp.concatenate([jnp.transpose(value[rows, 0:128]), jnp.transpose(value[rows, 128:256])], 1)
        )
    return jnp.concatenate(blocks, 0)


def some_coils(sens, cot, w):
    coils = [sens[group, k] for group in range(sens.shape[0]) for k in range(2)]
    count = len(coils)
    g_real, g_imag = cot[0], cot[1]
    real = jnp.concatenate([s[0] * g_real - s[1] * g_imag for s in coils], 0)
    imag = jnp.concatenate([s[0] * g_imag + s[1] * g_real for s in coils], 0)
    forward = (w.tables[2], w.tables[3])
    backward = (w.tables[0], w.tables[1])
    value = turned(product3(split2(jnp.concatenate([real, imag], 1)), forward), count)
    value = product3(split2(value), forward)
    kept = jnp.concatenate([w.kept[...]] * count, 0)
    value = value * jnp.concatenate([kept, kept], 1)
    value = turned(product3(split2(value), backward), count)
    value = product3(split2(value), backward)
    real = sum(
        s[0] * value[128 * k : 128 * k + 128, 0:128] + s[1] * value[128 * k : 128 * k + 128, 128:256]
        for k, s in enumerate(coils)
    )
    imag = sum(
        s[0] * value[128 * k : 128 * k + 128, 128:256] - s[1] * value[128 * k : 128 * k + 128, 0:128]
        for k, s in enumerate(coils)
    )
    return real, imag


class Refs:
    def __init__(self, **refs):
        self.__dict__.update(refs)


WEIGHTS = dict(
    mask=((128, 128), jnp.int32),
    embed=((8, CHANNELS), F32),
    gain=((1, CHANNELS), F32),
    qkv=((CHANNELS, 288), BF16),
    proj=((CHANNELS, CHANNELS), BF16),
    unembed=((8, CHANNELS), F32),
    wide=((3, GROUPS, 8, 192), F32),
    narrow=((GROUPS, 32, 8), F32),
    tables=((4, 256, 256), BF16),
)
WORK = dict(
    pad=((128, 384), F32),
    gain_col=((CHANNELS, 128), F32),
    to_embed=((GROUPS, CHANNELS, 192), BF16),
    to_mixed=((GROUPS, CHANNELS, 192), BF16),
    from_embed=((2, GROUPS, 32, CHANNELS), BF16),
    qkv_t=((384, 128), BF16),
    turn=((128, 128), F32),
    field=((WINDOWS, 2, 32, 128), F32),
    label=((WINDOWS, 8, 128), F32),
    unit=((CHANNELS, TOKENS), F32),
    mixed=((CHANNELS, TOKENS), F32),
    d_proj=((288, TOKENS), F32),
    d_field=((WINDOWS, 32, 128), F32),
    kept=((128, 128), F32),
    line=((2, 128, 128), F32),
)
BUFFERS = (
    ((2, 2, 8, 16, 128), F32),
    ((8, 8, 64), jnp.int32),
    ((2, 8, 16, 128), F32),
    ((8, 2, 2, 128, 128), F32),
    ((2, 8, 16, 128), F32),
    ((2, 128, 128), F32),
    ((16, 2, 8, 128), F32),
    ((2, 4, 16, 128), F32),
    ((2, 8, 16, 128), F32),
    ((2, 8, 128, 128), F32),
)
SENDING = 7
EACH = 3
STRIDE = 45
VMEM_LIMIT = 60 * 1024 * 1024
SLABS = 16
COILS = 8
BATCH = 4
RING = 4


def kernel(image, cot, sens, labels, *rest):
    weights = rest[: len(WEIGHTS)]
    out = rest[len(WEIGHTS)]
    held = rest[len(WEIGHTS) + 1 : 2 * len(WEIGHTS) + 1]
    scratch = rest[2 * len(WEIGHTS) + 1 :]
    w = Refs(**dict(zip(WEIGHTS, held)), **dict(zip(WORK, scratch)))
    (col, lab, piece, sens_all, own_cot, cot_all, line_parts, halo, final, gathered) = (
        scratch[len(WORK) : len(WORK) + len(BUFFERS)]
    )
    sems, sens_sem, ag_sems, ready = scratch[len(WORK) + len(BUFFERS) :]
    (own_sem, field_sem, col_sem, cot_sem, line_sem, halo_sem, out_sem, send_sem, sens_send_sem) = [
        sems.at[i] for i in range(9)
    ]
    y_sem, right_sem, left_sem, far_sem, right2_sem, left2_sem, far2_sem = [ag_sems.at[i] for i in range(7)]
    s = lax.axis_index("slab")
    c = lax.axis_index("coil")
    sends = []

    def send(source, target, recv, device):
        copy = pltpu.make_async_remote_copy(
            src_ref=source, dst_ref=target, send_sem=send_sem, recv_sem=recv,
            device_id=device, device_id_type=MESH,
        )
        copy.start()
        sends.append(copy)

    def local(source, target, sem):
        pltpu.make_async_copy(source, target, sem).start()

    def await_bytes(ref, sem):
        pltpu.make_async_copy(ref, ref, sem).wait()

    def span(start, size, step):
        return pl.ds(pl.multiple_of(start, step), size)

    barrier = pltpu.get_barrier_semaphore()
    for d in range(1, SLABS):
        pl.semaphore_signal(barrier, inc=1, device_id={"slab": lax.rem(s + d, SLABS)}, device_id_type=MESH)
    for d in range(1, COILS):
        pl.semaphore_signal(barrier, inc=1, device_id={"coil": lax.rem(c + d, COILS)}, device_id_type=MESH)
    halves = [span(lax.rem(16 * c + 8 + 8 * half, 128), 8, 8) for half in range(2)]
    places = [slice(8 * half, 8 * half + 8) for half in range(2)]
    for xs, place in zip(halves, places):
        local(cot.at[:, :, xs, :], own_cot.at[:, :, place, :], field_sem)
    for source, target in zip(weights, held):
        local(source, target, own_sem)
    local(labels.at[:, span(8 * c, 8, 8), :], lab, own_sem)
    for arr, field in enumerate((image, cot)):
        for xs, place in zip(halves, places):
            local(field.at[:, 4:8, xs, :], col.at[arr, :, 0:4, place, :], col_sem)
    pl.semaphore_wait(barrier, SLABS + COILS - 2)
    for d in range(1, SLABS):
        pl.semaphore_signal(ready, inc=1, device_id={"slab": lax.rem(s + d, SLABS)}, device_id_type=MESH)
    mine = pl.ds(pl.multiple_of(8 * s, 8), 8)
    for d in range(1, SLABS):
        t = lax.rem(s + d, SLABS)
        send(cot.at[:, :, lax.rem(16 * c + 8 + t, 128), :], cot_all.at[:, mine, :], cot_sem, {"slab": t})
    local(cot.at[:, :, lax.rem(16 * c + 8 + s, 128), :], cot_all.at[:, mine, :], cot_sem)
    below = lax.rem(s + SLABS - 1, SLABS)
    above = lax.rem(s + 1, SLABS)
    for arr, field in enumerate((image, cot)):
        for xs, place in zip(halves, places):
            send(field.at[:, 0:4, xs, :], col.at[arr, :, 4:8, place, :], col_sem, {"slab": below})

    def send_line(slab, coil):
        pltpu.make_async_remote_copy(
            src_ref=sens.at[:, :, :, lax.rem(16 * coil + 8 + slab, 128), :],
            dst_ref=sens_all.at[c, :, :, mine, :],
            send_sem=sens_send_sem,
            recv_sem=sens_sem.at[c],
            device_id={"slab": slab, "coil": coil},
            device_id_type=MESH,
        ).start()

    local(sens.at[:, :, :, lax.rem(16 * c + 8 + s, 128), :], sens_all.at[c, :, :, mine, :], sens_sem.at[c])
    pl.semaphore_wait(ready, SLABS - 1)

    others = SLABS * COILS - 1
    share = EACH * HEADS * (TOKENS // CHUNK)

    def send_other(k):
        d = lax.rem(STRIDE * k + 7, others) + 1
        send_line(lax.rem(s + lax.rem(d, SLABS), SLABS), lax.rem(c + d // SLABS, COILS))

    for k in range(others - share * SENDING):
        send_other(k)

    for target in held:
        await_bytes(target, own_sem)
    await_bytes(lab, own_sem)
    prepare_weights(w)
    w.kept[...] = jnp.transpose(w.mask[...].astype(F32))
    await_bytes(col, col_sem)
    prepare_fields(col, lab, w)

    def windows(first, last):
        lax.fori_loop(first, last, lambda win, carry: (one_window(win, w), carry)[1], 0)

    def window_and_sends(win, carry):
        first = others - share * SENDING + share * win

        def beside(step):
            for k in range(EACH):
                send_other(first + EACH * step + k)

        one_window(win, w, beside)
        return carry

    lax.fori_loop(0, SENDING, window_and_sends, 0)
    await_bytes(cot_all, cot_sem)
    w.line[...] = jnp.zeros((2, 128, 128), F32)
    for first in range(0, COILS, BATCH):
        for group in range(first, first + BATCH):
            await_bytes(sens_all.at[group], sens_sem.at[group])
        real, imag = some_coils(sens_all.at[first : first + BATCH], cot_all, w)
        w.line[0] += real
        w.line[1] += imag
    for d in range(1, SLABS):
        t = lax.rem(s + d, SLABS)
        send(w.line.at[:, span(8 * t, 8, 8), :], line_parts.at[s], line_sem, {"slab": t})
    local(w.line.at[:, mine, :], line_parts.at[s], line_sem)
    windows(SENDING, WINDOWS)
    finish_fields(piece, w)
    send(piece.at[:, 4:8], halo, halo_sem, {"slab": above})
    await_bytes(line_parts, line_sem)
    rows = final.reshape(256, 128)
    parts = line_parts.reshape(16, 16, 128)
    for x in range(16):
        rows[pl.ds(x, 16, stride=16), :] = parts[x] * -STEP_SIZE
    await_bytes(own_cot, field_sem)
    final[...] = final[...] + own_cot[...]
    final[:, 4:8] = final[:, 4:8] + piece[:, 0:4]
    await_bytes(halo, halo_sem)
    final[:, 0:4] = final[:, 0:4] + halo[...]
    high = c // RING
    across = lax.rem(c, RING)
    right = RING * high + lax.rem(across + 1, RING)
    left = RING * high + lax.rem(across + RING - 1, RING)
    other = lax.rem(c + RING, COILS)

    def column(coil, half):
        return gathered.at[:, :, span(lax.rem(16 * coil + 8 + 8 * half, 128), 8, 8), :]

    def pass_on(coil, half, target, sem):
        block = column(coil, half)
        send(block, block, sem, {"coil": target})

    def keep(coil):
        for half in range(2):
            xs = span(lax.rem(16 * coil + 8 + 8 * half, 128), 8, 8)
            local(gathered.at[:, :, xs, :], out.at[:, :, xs, :], out_sem)

    for half in range(2):
        gathered[:, :, halves[half], :] = final[:, :, places[half], :]
    for half in range(2):
        pass_on(c, half, other, y_sem)
    for half in (0, 1):
        pass_on(c, half, right, right_sem)
        pass_on(c, 1 - half, left, left_sem)
    two = final.at[:, :, 0:16, :]
    one = final.at[:, :, 0:8, :]
    await_bytes(two, y_sem)
    await_bytes(two, right_sem)
    await_bytes(two, left_sem)
    pass_on(left, 0, right, far_sem)
    pass_on(right, 1, left, far_sem)
    across_right = lax.rem(right + RING, COILS)
    across_left = lax.rem(left + RING, COILS)
    for half in (0, 1):
        pass_on(other, half, right, right2_sem)
        pass_on(other, 1 - half, left, left2_sem)
    for coil in (c, other, right, left):
        keep(coil)
    await_bytes(two, right2_sem)
    await_bytes(two, left2_sem)
    pass_on(across_left, 0, right, far2_sem)
    pass_on(across_right, 1, left, far2_sem)
    keep(across_right)
    keep(across_left)
    far = RING * high + lax.rem(across + 2, RING)
    await_bytes(two, far_sem)
    keep(far)
    await_bytes(two, far2_sem)
    keep(lax.rem(far + RING, COILS))
    await_bytes(sens_all.at[0:7], sens_send_sem)
    await_bytes(sens_all.at[7, :, :, 0:120, :], sens_send_sem)
    await_bytes(out, out_sem)
    for copy in sends:
        copy.wait_send()


def body(image, cotangent, sens, mask, labels, embed_weight, ln_gain, qkv_weight, proj_weight, unembed_weight):
    wide, narrow = selections()
    anywhere = pl.BlockSpec(memory_space=pl.ANY)
    scratch = [pltpu.VMEM(shape, dtype) for held in (WEIGHTS, WORK) for shape, dtype in held.values()]
    scratch += [pltpu.VMEM(shape, dtype) for shape, dtype in BUFFERS]
    scratch += [
        pltpu.SemaphoreType.DMA((9,)),
        pltpu.SemaphoreType.DMA((COILS,)),
        pltpu.SemaphoreType.DMA((7,)),
        pltpu.SemaphoreType.REGULAR,
    ]
    return pl.pallas_call(
        kernel,
        out_shape=jax.ShapeDtypeStruct(image.shape, F32),
        in_specs=[anywhere] * (4 + len(WEIGHTS)),
        out_specs=anywhere,
        scratch_shapes=scratch,
        compiler_params=pltpu.CompilerParams(
            collective_id=0, has_side_effects=True, vmem_limit_bytes=VMEM_LIMIT
        ),
    )(
        image, cotangent, sens, labels, mask, embed_weight, ln_gain.reshape(1, CHANNELS), qkv_weight,
        proj_weight, unembed_weight.T, jnp.asarray(wide), jnp.asarray(narrow), jnp.asarray(dft_tables(128)),
    )


def solution(mesh):
    placed = (
        P(None, "slab", None, None),
        P(None, "slab", None, None),
        P("coil", None, "slab", None, None),
        P(),
        P("slab", None, None),
        P(),
        P(),
        P(),
        P(),
        P(),
    )
    return jax.shard_map(
        body, mesh=mesh, in_specs=placed, out_specs=P(None, "slab", None, None), check_vma=False
    )
```
